128 devices in a mesh: fibre: 16 (over x, y_lo, core), freq: 8 (over z, y_hi).
Axes of the slice: x: 4, y: 4 (y_hi: 2, y_lo: 2; y = y_hi * 2 + y_lo), z: 4, core: 2. Of those that a mesh axis runs over, the one named last changes fastest.
Arguments:
- records: bfloat16 [48, 6000, 2048], P('freq', 'fibre'), may hold values from -6 to 6
- channel_live: int32 [2048], P('fibre'), may hold values 0 or 1
- offset_limit: int32 [2048], P('fibre'), may hold values from 1 to 64
Outputs:
- stacked: float32 [64, 2, 512, 2048], P(None, None, 'freq', 'fibre')
The draws below stay inside these ranges and needn't reach their ends.
All inputs are finite; a program needn't handle non-finite values. No bound on the sum of `channel_live` on one device may be relied on, other than what follows from the above.
Results may differ from the reference program's by a relative error of at most 0.0055.
Values may be sent and summed in bfloat16 or wider, within the bound.
No kernel may reach another device: no remote copies, remote signals or barrier semaphores. Data moves between devices by JAX's collectives and lax.ppermute only.
A program may use at most 128 MiB of HBM per device.

```python
import math
import jax
import jax.numpy as jnp
from jax import lax

CH = 2048
SAMPLES = 6000
NB = 512
HALF = 32
FIRST_BIN = 60
OFFSETS = 64
WINDOWS = 48


def place_ends(drawn, stream_key, smallest, high):
    longest = drawn.shape.index(max(drawn.shape))
    spots = []
    for shift in (0, 1):
        where = [jax.random.randint(jax.random.fold_in(stream_key, axis), (), 0, length) for axis, length in enumerate(drawn.shape)]
        where[longest] = (where[longest] + shift) % drawn.shape[longest]
        spots.append(tuple(where))
    return drawn.at[spots[0]].set(smallest).at[spots[1]].set(high)


def shard_levels(key, shape, cuts, least, largest):
    def one(dim, shards_of):
        draws = jax.random.uniform(jax.random.fold_in(jax.random.fold_in(key, 6), dim), (shards_of,), jnp.float32, least / len(cuts), largest / len(cuts))
        return jnp.repeat(jnp.exp(draws), shape[dim] // shards_of).reshape((-1,) + (1,) * (len(shape) - dim - 1))

    gain = one(*cuts[0])
    for cut in cuts[1:]:
        gain = gain * one(*cut)
    return gain


def noise(stream_key, dims, spread, bound, pieces=(), held_as=jnp.bfloat16):
    values = spread * jax.random.normal(stream_key, dims, jnp.float32)
    if pieces:
        values = values * shard_levels(stream_key, dims, pieces, -0.22, 0.18)
    return jnp.clip(values, -bound, bound).astype(held_as)


def setup_inputs(seed: int = 0) -> dict:
    splits = jax.random.split(jax.random.key(seed), 4)
    return {
        "records": noise(splits[0], (WINDOWS, SAMPLES, CH), 1.0, 6.0, ((0, 8), (1, 16))),
        "channel_live": place_ends((jax.random.randint(splits[1], (CH,), 0, 8) < 7).astype(jnp.int32), jax.random.fold_in(splits[1], 1), 0, 1),
        "offset_limit": place_ends(jax.random.randint(splits[2], (CH,), 1, OFFSETS + 1), jax.random.fold_in(splits[2], 1), 1, OFFSETS).astype(jnp.int32),
    }


def make_table(samples, first, count):
    steps = lax.iota(jnp.int32, samples)[:, None]
    bins = first + lax.iota(jnp.int32, count)[None, :]
    phase = (steps * bins % samples).astype(jnp.float32) * (2.0 * math.pi / samples)
    taper = 0.5 - 0.5 * jnp.cos(steps.astype(jnp.float32) * (2.0 * math.pi / samples))
    return jnp.concatenate([taper * jnp.cos(phase), -taper * jnp.sin(phase)], axis=1).astype(jnp.bfloat16)

def whiten(spectra, live, kept, margin):
    extent = kept + 2 * margin
    real_part = spectra[:, :extent]
    imag_part = spectra[:, extent:]
    amplitude = jnp.sqrt(real_part * real_part + imag_part * imag_part)
    rows = lax.iota(jnp.int32, kept)[:, None]
    cols = lax.iota(jnp.int32, extent)[None, :]
    band = jnp.where((cols >= rows) & (cols <= rows + 2 * margin), 1.0 / (2 * margin + 1), 0.0).astype(jnp.float32)
    smooth = jnp.einsum('bj,wjc->wbc', band, amplitude, precision=lax.Precision.HIGHEST)
    scale = live[None, None, :] / (smooth + 1e-06)
    white = jnp.stack([real_part[:, margin:margin + kept] * scale, imag_part[:, margin:margin + kept] * scale], axis=1)
    return white.astype(jnp.bfloat16)

def cross_spectra(local, extended, count):
    width = local.shape[3]
    first_re = local[:, 0].astype(jnp.float32)
    first_im = local[:, 1].astype(jnp.float32)

    def one_offset(shift):
        partner = lax.dynamic_slice_in_dim(extended, shift + 1, width, 3)
        second_re = partner[:, 0].astype(jnp.float32)
        second_im = partner[:, 1].astype(jnp.float32)
        real_sum = lax.optimization_barrier(jnp.sum(first_re * second_re + first_im * second_im, axis=0))
        imag_sum = lax.optimization_barrier(jnp.sum(first_im * second_re - first_re * second_im, axis=0))
        return jnp.stack([real_sum, imag_sum], axis=0)
    return lax.map(one_offset, lax.iota(jnp.int32, count))

def reference(records, channel_live, offset_limit):
    table = make_table(SAMPLES, FIRST_BIN, NB + 2 * HALF)
    spectra = jnp.einsum('sj,wsc->wjc', table.astype(jnp.float32), records.astype(jnp.float32))
    white = whiten(spectra, channel_live.astype(jnp.float32), NB, HALF)
    padding = jnp.zeros(white.shape[:3] + (OFFSETS,), jnp.bfloat16)
    extended = jnp.concatenate([white, padding], axis=3)
    cross = cross_spectra(white, extended, OFFSETS)
    keep = (lax.iota(jnp.int32, OFFSETS)[:, None] + 1 <= offset_limit[None, :]).astype(jnp.float32)
    return cross * keep[:, None, None, :]
```

```python
import functools

import jax
import jax.numpy as jnp
import numpy as np
from jax import lax
from jax.experimental import pallas as pl
from jax.experimental.pallas import tpu as pltpu
from jax.sharding import PartitionSpec as P

SAMPLES = 6000
NB = 512
HALF = 32
FIRST_BIN = 60
OFFSETS = 64
BINS = NB + 2 * HALF
RANK = 96
LANES = 128
F32 = jnp.float32
BF16 = jnp.bfloat16


def split_pair(values):
    high = values.astype(jnp.bfloat16)
    low = (values - high.astype(np.float64)).astype(jnp.bfloat16)
    return high, low


def make_tables(parts):
    run = SAMPLES // parts
    times = np.arange(run) - (run - 1) / 2
    bins = np.arange(FIRST_BIN - 1, FIRST_BIN + BINS + 1)
    weight = 1.0 + np.arange(len(bins)) / len(bins)
    angles = 2.0 * np.pi * np.outer(times, bins) / SAMPLES
    rows = []
    for wave in (np.cos, np.sin):
        vectors = np.linalg.svd(wave(angles) * weight, full_matrices=False)[0]
        vectors = vectors[:, : RANK // 2]
        rows.append((vectors * np.sign(vectors[run // 2 + 3])).T)
    down = np.concatenate(rows)
    samples = np.arange(SAMPLES)
    kept = np.arange(FIRST_BIN, FIRST_BIN + BINS)
    taper = 0.5 - 0.5 * np.cos(2.0 * np.pi * samples / SAMPLES)
    phase = 2.0 * np.pi * (np.outer(samples, kept) % SAMPLES) / SAMPLES
    table = np.concatenate([np.cos(phase), -np.sin(phase)], axis=1) * taper[:, None]
    back = np.einsum("psj,rs->jpr", table.reshape(parts, run, 2 * BINS), down)
    return down, back.reshape(2 * BINS, parts * RANK)


def project_kernel(down_ref, records_ref, out_ref):
    parts = out_ref.shape[0]
    wide = 4
    for start in range(0, parts, wide):
        block = records_ref[0, :, start * LANES : (start + wide) * LANES]
        both = jnp.dot(down_ref[...], block, preferred_element_type=F32)
        sums = (both[:RANK] + both[RANK:]).astype(BF16)
        for part in range(wide):
            out_ref[start + part, 0] = sums[:, part * LANES : (part + 1) * LANES]


def project(down, records, parts):
    windows, run, channels = records.shape
    return pl.pallas_call(
        project_kernel,
        grid=(windows,),
        in_specs=[
            pl.BlockSpec((2 * RANK, run), lambda w: (0, 0)),
            pl.BlockSpec((1, run, channels), lambda w: (w, 0, 0)),
        ],
        out_specs=pl.BlockSpec((parts, 1, RANK, LANES), lambda w: (0, w, 0, 0)),
        out_shape=jax.ShapeDtypeStruct((parts, windows, RANK, LANES), BF16),
        compiler_params=pltpu.CompilerParams(vmem_limit_bytes=40 * 2**20),
        cost_estimate=pl.CostEstimate(
            flops=4 * RANK * run * channels * windows,
            bytes_accessed=2 * records.size + 2 * parts * windows * RANK * LANES,
            transcendentals=0,
        ),
        name="project",
    )(down, records)


def up_by(values, rows):
    return pltpu.roll(values, values.shape[0] - rows, axis=0)


def whiten_kernel(live_ref, back_ref, sums_ref, first_ref, second_ref):
    parts = sums_ref.shape[0]
    columns = jnp.concatenate(
        [sums_ref[:, i].reshape(parts * RANK, LANES) for i in range(2)], axis=1
    )
    spectra = jnp.dot(back_ref[...], columns, preferred_element_type=F32)
    real_part = spectra[:BINS]
    imag_part = spectra[BINS:]
    amplitude = jnp.sqrt(real_part * real_part + imag_part * imag_part)
    total = amplitude
    for reach in (1, 2, 4):
        total = total + up_by(total, reach)
    for reach in (8, 16, 32):
        total = total[: total.shape[0] - reach] + total[reach:]
    smooth = (total[:NB] + amplitude[2 * HALF :]) * (1.0 / (2 * HALF + 1))
    live = live_ref[...].astype(F32)
    scale = jnp.concatenate([live, live], axis=1) / (smooth + 1e-06)
    real_part = real_part[HALF : HALF + NB] * scale
    imag_part = imag_part[HALF : HALF + NB] * scale
    groups = first_ref.shape[0]
    left = lax.broadcasted_iota(jnp.int32, (NB, LANES), 1) < LANES // 2
    for i in range(2):
        real_one = real_part[:, i * LANES : (i + 1) * LANES]
        imag_one = imag_part[:, i * LANES : (i + 1) * LANES]
        first = jnp.where(left, real_one, pltpu.roll(imag_one, LANES // 2, axis=1))
        second = jnp.where(left, pltpu.roll(real_one, LANES // 2, axis=1), imag_one)
        first_ref[:, i] = first.astype(BF16).reshape(groups, NB // groups, LANES)
        second_ref[:, i] = second.astype(BF16).reshape(groups, NB // groups, LANES)


def whiten(live, back, sums, groups):
    parts, windows = sums.shape[:2]
    shape = (groups, windows, NB // groups, LANES)
    half = pl.BlockSpec((groups, 2, NB // groups, LANES), lambda w: (0, w, 0, 0))
    return pl.pallas_call(
        whiten_kernel,
        grid=(windows // 2,),
        in_specs=[
            pl.BlockSpec((1, LANES), lambda w: (0, 0)),
            pl.BlockSpec(back.shape, lambda w: (0, 0)),
            pl.BlockSpec((parts, 2, RANK, LANES), lambda w: (0, w, 0, 0)),
        ],
        out_specs=[half, half],
        out_shape=[jax.ShapeDtypeStruct(shape, BF16)] * 2,
        compiler_params=pltpu.CompilerParams(vmem_limit_bytes=48 * 2**20),
        cost_estimate=pl.CostEstimate(
            flops=2 * back.size * windows * LANES,
            bytes_accessed=2 * (back.size + sums.size + 2 * windows * NB * LANES),
            transcendentals=0,
        ),
        name="whiten",
    )(live, back, sums)


def cross_kernel(limit_ref, first_ref, second_ref, next_ref, out_ref, real_own, imag_own, real_next, imag_next):
    groups, windows, bins, _ = first_ref.shape
    every = groups * windows
    half = LANES // 2
    left = lax.broadcasted_iota(jnp.int32, (every * bins, LANES), 1) < half
    first = first_ref[...].astype(F32).reshape(every * bins, LANES)
    second = second_ref[...].astype(F32).reshape(every * bins, LANES)
    real_own[...] = jnp.where(left, first, pltpu.roll(second, half, axis=1))
    imag_own[...] = jnp.where(left, pltpu.roll(first, half, axis=1), second)
    after = next_ref[...].astype(F32).reshape(every * bins, LANES)
    real_next[...] = after
    imag_next[...] = pltpu.roll(after, half, axis=1)
    offsets = lax.broadcasted_iota(jnp.int32, (OFFSETS, LANES), 0) + 1
    keep = (offsets <= limit_ref[...]).astype(F32)
    lane = lax.broadcasted_iota(jnp.int32, (LANES, LANES), 1)

    def skewed(gram):
        for bit in (64, 32, 16, 8):
            rows = gram.shape[0] - bit
            if bit == 64:
                rows = 128
            gram = jnp.where((lane[:rows] & bit) != 0, gram[bit : bit + rows], gram[:rows])
        for bit in (4, 2, 1):
            gram = jnp.where((lane[: gram.shape[0]] & bit) != 0, up_by(gram, bit), gram)
        return up_by(gram, 1)[:OFFSETS]

    @pl.loop(0, bins)
    def _(index):
        rows = pl.ds(index, every, stride=bins)
        real_x = real_own[rows, :]
        imag_x = imag_own[rows, :]
        real_y = jnp.concatenate([real_x, real_next[rows, :]], axis=1)
        imag_y = jnp.concatenate([imag_x, imag_next[rows, :]], axis=1)
        partner = jnp.concatenate([real_y, imag_y], axis=0).T[: LANES + OFFSETS].astype(BF16)
        own = jnp.concatenate(
            [
                jnp.concatenate([real_x, imag_x], axis=1),
                jnp.concatenate([imag_x, -real_x], axis=1),
            ],
            axis=0,
        ).astype(BF16)
        gram = jnp.dot(partner, own, preferred_element_type=F32)
        for part in range(2):
            value = skewed(gram[:, part * LANES : (part + 1) * LANES]) * keep
            out_ref[:, part, pl.ds(index, 1), :] = value[:, None, :]


def cross_spectra(limit, first, second, after):
    groups, windows, bins, _ = first.shape
    step = 16
    half = pl.BlockSpec((groups, windows, step, LANES), lambda b: (0, 0, b, 0))
    scratch = pltpu.VMEM((groups * windows * step, LANES), F32)
    return pl.pallas_call(
        cross_kernel,
        grid=(bins // step,),
        in_specs=[pl.BlockSpec((1, LANES), lambda b: (0, 0)), half, half, half],
        out_specs=pl.BlockSpec((OFFSETS, 2, step, LANES), lambda b: (0, 0, b, 0)),
        out_shape=jax.ShapeDtypeStruct((OFFSETS, 2, bins, LANES), F32),
        scratch_shapes=[scratch] * 4,
        compiler_params=pltpu.CompilerParams(vmem_limit_bytes=40 * 2**20),
        cost_estimate=pl.CostEstimate(
            flops=2 * bins * 192 * 96 * 256,
            bytes_accessed=6 * first.size + 4 * OFFSETS * 2 * bins * LANES,
            transcendentals=0,
        ),
        name="cross_spectra",
    )(limit, first, second, after)


def body(down, back, records, channel_live, offset_limit):
    parts = lax.axis_size("fibre")
    groups = lax.axis_size("freq")
    sums = project(down, records, parts)
    sums = lax.all_to_all(sums, "fibre", split_axis=0, concat_axis=0, tiled=True)
    first, second = whiten(channel_live[None, :], back, sums, groups)
    first = lax.all_to_all(first, "freq", split_axis=0, concat_axis=0, tiled=True)
    after = lax.ppermute(first, "fibre", [(i, i - 1) for i in range(1, parts)])
    second = lax.all_to_all(second, "freq", split_axis=0, concat_axis=0, tiled=True)
    return cross_spectra(offset_limit[None, :], first, second, after)


def solution(mesh):
    down, back = make_tables(mesh.shape["fibre"])
    down = np.concatenate(split_pair(down))
    back = split_pair(back)[0]
    return jax.shard_map(
        functools.partial(body, down, back),
        mesh=mesh,
        in_specs=(P("freq", "fibre", None), P("fibre"), P("fibre")),
        out_specs=P(None, None, "freq", "fibre"),
        check_vma=False,
    )
```

```python
import functools

import jax
import jax.numpy as jnp
import numpy as np
from jax import lax
from jax.experimental import pallas as pl
from jax.experimental.pallas import tpu as pltpu
from jax.sharding import PartitionSpec as P

SAMPLES = 6000
NB = 512
HALF = 32
FIRST_BIN = 60
OFFSETS = 64
BINS = NB + 2 * HALF
RANK = 96
LANES = 128
F32 = jnp.float32
BF16 = jnp.bfloat16


def split_pair(values):
    high = values.astype(jnp.bfloat16)
    low = (values - high.astype(np.float64)).astype(jnp.bfloat16)
    return high, low


def make_tables(parts):
    run = SAMPLES // parts
    times = np.arange(run) - (run - 1) / 2
    bins = np.arange(FIRST_BIN - 1, FIRST_BIN + BINS + 1)
    weight = 1.0 + np.arange(len(bins)) / len(bins)
    angles = 2.0 * np.pi * np.outer(times, bins) / SAMPLES
    rows = []
    for wave in (np.cos, np.sin):
        vectors = np.linalg.svd(wave(angles) * weight, full_matrices=False)[0]
        vectors = vectors[:, : RANK // 2]
        rows.append((vectors * np.sign(vectors[run // 2 + 3])).T)
    down = np.concatenate(rows)
    samples = np.arange(SAMPLES)
    kept = np.arange(FIRST_BIN, FIRST_BIN + BINS)
    taper = 0.5 - 0.5 * np.cos(2.0 * np.pi * samples / SAMPLES)
    phase = 2.0 * np.pi * (np.outer(samples, kept) % SAMPLES) / SAMPLES
    table = np.concatenate([np.cos(phase), -np.sin(phase)], axis=1) * taper[:, None]
    back = np.einsum("psj,rs->jpr", table.reshape(parts, run, 2 * BINS), down)
    return down, back.reshape(2 * BINS, parts * RANK)


def project_kernel(down_ref, records_ref, out_ref):
    parts = out_ref.shape[0]
    wide = 4
    for start in range(0, parts, wide):
        block = records_ref[0, :, start * LANES : (start + wide) * LANES]
        both = jnp.dot(down_ref[...], block, preferred_element_type=F32)
        sums = (both[:RANK] + both[RANK:]).astype(BF16)
        for part in range(wide):
            out_ref[start + part, 0] = sums[:, part * LANES : (part + 1) * LANES]


def project(down, records, parts):
    windows, run, channels = records.shape
    return pl.pallas_call(
        project_kernel,
        grid=(windows,),
        in_specs=[
            pl.BlockSpec((2 * RANK, run), lambda w: (0, 0)),
            pl.BlockSpec((1, run, channels), lambda w: (w, 0, 0)),
        ],
        out_specs=pl.BlockSpec((parts, 1, RANK, LANES), lambda w: (0, w, 0, 0)),
        out_shape=jax.ShapeDtypeStruct((parts, windows, RANK, LANES), BF16),
        compiler_params=pltpu.CompilerParams(vmem_limit_bytes=56 * 2**20),
        cost_estimate=pl.CostEstimate(
            flops=4 * RANK * run * channels * windows,
            bytes_accessed=2 * records.size + 2 * parts * windows * RANK * LANES,
            transcendentals=0,
        ),
        name="project",
    )(down, records)


def up_by(values, rows):
    return pltpu.roll(values, values.shape[0] - rows, axis=0)


def whiten_kernel(live_ref, back_ref, sums_ref, out_ref):
    parts = sums_ref.shape[0]
    columns = jnp.concatenate(
        [sums_ref[:, i].reshape(parts * RANK, LANES) for i in range(2)], axis=1
    )
    spectra = jnp.dot(back_ref[...], columns, preferred_element_type=F32)
    real_part = spectra[:BINS]
    imag_part = spectra[BINS:]
    amplitude = jnp.sqrt(real_part * real_part + imag_part * imag_part)
    total = amplitude
    for reach in (1, 2, 4):
        total = total + up_by(total, reach)
    for reach in (8, 16, 32):
        total = total[: total.shape[0] - reach] + total[reach:]
    smooth = (total[:NB] + amplitude[2 * HALF :]) * (1.0 / (2 * HALF + 1))
    live = live_ref[...].astype(F32)
    scale = jnp.concatenate([live, live], axis=1) / (smooth + 1e-06)
    real_part = real_part[HALF : HALF + NB] * scale
    imag_part = imag_part[HALF : HALF + NB] * scale
    groups = out_ref.shape[0]
    left = lax.broadcasted_iota(jnp.int32, (NB, LANES), 1) < LANES // 2
    for i in range(2):
        real_one = real_part[:, i * LANES : (i + 1) * LANES]
        imag_one = imag_part[:, i * LANES : (i + 1) * LANES]
        first = jnp.where(left, real_one, pltpu.roll(imag_one, LANES // 2, axis=1))
        second = jnp.where(left, pltpu.roll(real_one, LANES // 2, axis=1), imag_one)
        out_ref[:, 0, i] = first.astype(BF16).reshape(groups, NB // groups, LANES)
        out_ref[:, 1, i] = second.astype(BF16).reshape(groups, NB // groups, LANES)


def whiten(live, back, sums, groups):
    parts, windows = sums.shape[:2]
    shape = (groups, 2, windows, NB // groups, LANES)
    return pl.pallas_call(
        whiten_kernel,
        grid=(windows // 2,),
        in_specs=[
            pl.BlockSpec((1, LANES), lambda w: (0, 0)),
            pl.BlockSpec(back.shape, lambda w: (0, 0)),
            pl.BlockSpec((parts, 2, RANK, LANES), lambda w: (0, w, 0, 0)),
        ],
        out_specs=pl.BlockSpec((groups, 2, 2, NB // groups, LANES), lambda w: (0, 0, w, 0, 0)),
        out_shape=jax.ShapeDtypeStruct(shape, BF16),
        compiler_params=pltpu.CompilerParams(vmem_limit_bytes=28 * 2**20),
        cost_estimate=pl.CostEstimate(
            flops=2 * back.size * windows * LANES,
            bytes_accessed=2 * (back.size + sums.size + 2 * windows * NB * LANES),
            transcendentals=0,
        ),
        name="whiten",
    )(live, back, sums)


def cross_kernel(limit_ref, halves_ref, next_ref, out_ref, real_own, imag_own, real_next, imag_next):
    groups, windows, bins, _ = next_ref.shape
    every = groups * windows
    half = LANES // 2
    left = lax.broadcasted_iota(jnp.int32, (every * bins, LANES), 1) < half
    first = halves_ref[:, 0].astype(F32).reshape(every * bins, LANES)
    second = halves_ref[:, 1].astype(F32).reshape(every * bins, LANES)
    real_own[...] = jnp.where(left, first, pltpu.roll(second, half, axis=1))
    imag_own[...] = jnp.where(left, pltpu.roll(first, half, axis=1), second)
    after = next_ref[...].astype(F32).reshape(every * bins, LANES)
    real_next[...] = after
    imag_next[...] = pltpu.roll(after, half, axis=1)
    offsets = lax.broadcasted_iota(jnp.int32, (OFFSETS, LANES), 0) + 1
    keep = (offsets <= limit_ref[...]).astype(F32)
    lane = lax.broadcasted_iota(jnp.int32, (LANES, LANES), 1)

    def skewed(gram):
        for bit in (64, 32, 16, 8):
            rows = gram.shape[0] - bit
            if bit == 64:
                rows = 128
            gram = jnp.where((lane[:rows] & bit) != 0, gram[bit : bit + rows], gram[:rows])
        turn = (lane[:8] & 7) + 1
        spot = lax.broadcasted_iota(jnp.int32, (8, LANES), 0) + turn
        pieces = []
        for row in range(0, OFFSETS + 8, 8):
            pieces.append(jnp.take_along_axis(gram[row : row + 8], spot & 7, axis=0))
        merged = [jnp.where(spot < 8, pieces[p], pieces[p + 1]) for p in range(OFFSETS // 8)]
        return jnp.concatenate(merged, axis=0)

    @pl.loop(0, bins, unroll=16)
    def _(index):
        rows = pl.ds(index, every, stride=bins)
        real_x = real_own[rows, :]
        imag_x = imag_own[rows, :]
        real_y = jnp.concatenate([real_x, real_next[rows, :]], axis=1)
        imag_y = jnp.concatenate([imag_x, imag_next[rows, :]], axis=1)
        partner = jnp.concatenate([real_y, imag_y], axis=0).T[: LANES + OFFSETS].astype(BF16)
        own = jnp.concatenate(
            [
                jnp.concatenate([real_x, imag_x], axis=1),
                jnp.concatenate([imag_x, -real_x], axis=1),
            ],
            axis=0,
        ).astype(BF16)
        gram = jnp.dot(partner, own, preferred_element_type=F32)
        for part in range(2):
            value = skewed(gram[:, part * LANES : (part + 1) * LANES]) * keep
            flat = out_ref.reshape(OFFSETS * 2 * bins, LANES)
            flat[pl.ds(part * bins + index, OFFSETS, stride=2 * bins), :] = value


def cross_spectra(limit, halves, after):
    groups, windows, bins, _ = after.shape
    step = 16
    own = pl.BlockSpec((groups, 2, windows, step, LANES), lambda b: (0, 0, 0, b, 0))
    half = pl.BlockSpec((groups, windows, step, LANES), lambda b: (0, 0, b, 0))
    scratch = pltpu.VMEM((groups * windows * step, LANES), F32)
    return pl.pallas_call(
        cross_kernel,
        grid=(bins // step,),
        in_specs=[pl.BlockSpec((1, LANES), lambda b: (0, 0)), own, half],
        out_specs=pl.BlockSpec((OFFSETS, 2, step, LANES), lambda b: (0, 0, b, 0)),
        out_shape=jax.ShapeDtypeStruct((OFFSETS, 2, bins, LANES), F32),
        scratch_shapes=[scratch] * 4,
        compiler_params=pltpu.CompilerParams(vmem_limit_bytes=20 * 2**20),
        cost_estimate=pl.CostEstimate(
            flops=2 * bins * 192 * 96 * 256,
            bytes_accessed=6 * after.size + 4 * OFFSETS * 2 * bins * LANES,
            transcendentals=0,
        ),
        name="cross_spectra",
    )(limit, halves, after)


def body(down, back, records, channel_live, offset_limit):
    parts = lax.axis_size("fibre")
    groups = lax.axis_size("freq")
    sums = project(down, records, parts)
    sums = lax.all_to_all(sums, "fibre", split_axis=0, concat_axis=0, tiled=True)
    halves = whiten(channel_live[None, :], back, sums, groups)
    halves = lax.all_to_all(halves, "freq", split_axis=0, concat_axis=0, tiled=True)
    after = lax.ppermute(halves[:, 0], "fibre", [(i, i - 1) for i in range(1, parts)])
    return cross_spectra(offset_limit[None, :], halves, after)


def solution(mesh):
    down, back = make_tables(mesh.shape["fibre"])
    down = np.concatenate(split_pair(down))
    back = split_pair(back)[0]
    return jax.shard_map(
        functools.partial(body, down, back),
        mesh=mesh,
        in_specs=(P("freq", "fibre", None), P("fibre"), P("fibre")),
        out_specs=P(None, None, "freq", "fibre"),
        check_vma=False,
    )
```

```python
import functools

import jax
import jax.numpy as jnp
import numpy as np
from jax import lax
from jax.experimental import pallas as pl
from jax.experimental.pallas import tpu as pltpu
from jax.sharding import PartitionSpec as P

SAMPLES = 6000
NB = 512
HALF = 32
FIRST_BIN = 60
OFFSETS = 64
BINS = NB + 2 * HALF
RANK = 96
PITCH = 24
LANES = 128
F32 = jnp.float32
BF16 = jnp.bfloat16


def split_pair(values):
    high = values.astype(jnp.bfloat16)
    low = (values - high.astype(np.float64)).astype(jnp.bfloat16)
    return high, low


def make_tables(parts):
    run = SAMPLES // parts
    times = np.arange(run) - (run - 1) / 2
    bins = np.arange(FIRST_BIN - 1, FIRST_BIN + BINS + 1)
    weight = 1.0 + np.arange(len(bins)) / len(bins)
    angles = 2.0 * np.pi * np.outer(times, bins) / SAMPLES
    rows = []
    for wave in (np.cos, np.sin):
        vectors = np.linalg.svd(wave(angles) * weight, full_matrices=False)[0]
        vectors = vectors[:, : RANK // 2]
        rows.append((vectors * np.sign(vectors[run // 2 + 3])).T)
    down = np.concatenate(rows)
    samples = np.arange(SAMPLES)
    kept = np.arange(FIRST_BIN, FIRST_BIN + BINS)
    taper = 0.5 - 0.5 * np.cos(2.0 * np.pi * samples / SAMPLES)
    phase = 2.0 * np.pi * (np.outer(samples, kept) % SAMPLES) / SAMPLES
    table = np.concatenate([np.cos(phase), -np.sin(phase)], axis=1) * taper[:, None]
    back = np.einsum("psj,rs->jpr", table.reshape(parts, run, 2 * BINS), down)
    return down, back.reshape(2 * BINS, parts * RANK)


def project_kernel(down_ref, records_ref, out_ref, held, arrived):
    parts, windows = out_ref.shape[:2]
    wide = 4

    def fetch(window):
        return pltpu.make_async_copy(records_ref.at[window], held.at[window], arrived.at[window])

    for window in range(windows):
        fetch(window).start()
    for window in range(windows):
        fetch(window).wait()
        for start in range(0, parts, wide):
            block = held[window, :, start * LANES : (start + wide) * LANES]
            both = jnp.dot(down_ref[...], block, preferred_element_type=F32)
            sums = (both[:RANK] + both[RANK:]).astype(BF16)
            for part in range(wide):
                out_ref[start + part, window] = sums[:, part * LANES : (part + 1) * LANES]


def project(down, records, parts):
    windows, run, channels = records.shape
    return pl.pallas_call(
        project_kernel,
        in_specs=[
            pl.BlockSpec(memory_space=pltpu.VMEM),
            pl.BlockSpec(memory_space=pltpu.HBM),
        ],
        out_specs=pl.BlockSpec(memory_space=pltpu.VMEM),
        out_shape=jax.ShapeDtypeStruct((parts, windows, RANK, LANES), BF16),
        scratch_shapes=[
            pltpu.VMEM(records.shape, BF16),
            pltpu.SemaphoreType.DMA((windows,)),
        ],
        compiler_params=pltpu.CompilerParams(vmem_limit_bytes=56 * 2**20),
        cost_estimate=pl.CostEstimate(
            flops=4 * RANK * run * channels * windows,
            bytes_accessed=2 * records.size + 2 * parts * windows * RANK * LANES,
            transcendentals=0,
        ),
        name="project",
    )(down, records)


def up_by(values, rows):
    return pltpu.roll(values, values.shape[0] - rows, axis=0)


def whiten_kernel(live_ref, back_ref, sums_ref, out_ref):
    parts = sums_ref.shape[0]
    columns = jnp.concatenate(
        [sums_ref[:, i].reshape(parts * RANK, LANES) for i in range(2)], axis=1
    )
    spectra = jnp.dot(back_ref[...], columns, preferred_element_type=F32)
    real_part = spectra[:BINS]
    imag_part = spectra[BINS:]
    amplitude = jnp.sqrt(real_part * real_part + imag_part * imag_part)
    total = amplitude
    for reach in (1, 2, 4):
        total = total + up_by(total, reach)
    for reach in (8, 16, 32):
        total = total[: total.shape[0] - reach] + total[reach:]
    smooth = (total[:NB] + amplitude[2 * HALF :]) * (1.0 / (2 * HALF + 1))
    live = live_ref[...].astype(F32)
    scale = jnp.concatenate([live, live], axis=1) / (smooth + 1e-06)
    real_part = real_part[HALF : HALF + NB] * scale
    imag_part = imag_part[HALF : HALF + NB] * scale
    groups = out_ref.shape[0]
    left = lax.broadcasted_iota(jnp.int32, (NB, LANES), 1) < LANES // 2
    for i in range(2):
        real_one = real_part[:, i * LANES : (i + 1) * LANES]
        imag_one = imag_part[:, i * LANES : (i + 1) * LANES]
        first = jnp.where(left, real_one, pltpu.roll(imag_one, LANES // 2, axis=1))
        second = jnp.where(left, pltpu.roll(real_one, LANES // 2, axis=1), imag_one)
        out_ref[:, 0, i] = first.astype(BF16).reshape(groups, NB // groups, LANES)
        out_ref[:, 1, i] = second.astype(BF16).reshape(groups, NB // groups, LANES)


def whiten(live, back, sums, groups):
    parts, windows = sums.shape[:2]
    shape = (groups, 2, windows, NB // groups, LANES)
    return pl.pallas_call(
        whiten_kernel,
        grid=(windows // 2,),
        in_specs=[
            pl.BlockSpec((1, LANES), lambda w: (0, 0)),
            pl.BlockSpec(back.shape, lambda w: (0, 0)),
            pl.BlockSpec((parts, 2, RANK, LANES), lambda w: (0, w, 0, 0)),
        ],
        out_specs=pl.BlockSpec((groups, 2, 2, NB // groups, LANES), lambda w: (0, 0, w, 0, 0)),
        out_shape=jax.ShapeDtypeStruct(shape, BF16),
        compiler_params=pltpu.CompilerParams(vmem_limit_bytes=28 * 2**20),
        cost_estimate=pl.CostEstimate(
            flops=2 * back.size * windows * LANES,
            bytes_accessed=2 * (back.size + sums.size + 2 * windows * NB * LANES),
            transcendentals=0,
        ),
        name="whiten",
    )(live, back, sums)


def swapped(tiles):
    row = lax.broadcasted_iota(jnp.int32, (8, LANES), 0)
    moved = [tiles[0]] + [pltpu.roll(tiles[j], j, axis=0) for j in range(1, 8)]
    for bit in (1, 2, 4):
        take = (row & bit) != 0
        moved = [jnp.where(take, moved[(j + bit) % 8], moved[j]) for j in range(8)]
    return [moved[0]] + [pltpu.roll(moved[8 - i], 8 - i, axis=0) for i in range(1, 8)]


def own_kernel(limit_ref, halves_ref, part_ref, later_ref, first_all, second_all):
    groups, _, windows, bins, _ = halves_ref.shape
    every = groups * windows
    half = LANES // 2
    first_all[:, :bins] = halves_ref[:, 0].astype(F32).reshape(every, bins, LANES)
    second_all[:, :bins] = halves_ref[:, 1].astype(F32).reshape(every, bins, LANES)
    first_rows = first_all.reshape(every * PITCH, LANES)
    second_rows = second_all.reshape(every * PITCH, LANES)
    left = lax.broadcasted_iota(jnp.int32, (every, LANES), 1) < half
    offsets = lax.broadcasted_iota(jnp.int32, (OFFSETS, LANES), 0) + 1
    keep = (offsets <= limit_ref[...]).astype(F32)
    lane = lax.broadcasted_iota(jnp.int32, (LANES, LANES), 1)
    turn = (lane[:8] & 7) + 1
    spot = lax.broadcasted_iota(jnp.int32, (8, LANES), 0) + turn

    def skewed(gram):
        gram = jnp.concatenate([gram, jnp.zeros((OFFSETS, LANES), F32)], axis=0)
        for bit in (64, 32, 16, 8):
            rows = min(gram.shape[0] - bit, LANES)
            gram = jnp.where((lane[:rows] & bit) != 0, gram[bit : bit + rows], gram[:rows])
        pieces = [
            jnp.take_along_axis(gram[row : row + 8], spot & 7, axis=0)
            for row in range(0, OFFSETS + 8, 8)
        ]
        merged = [jnp.where(spot < 8, pieces[p], pieces[p + 1]) for p in range(OFFSETS // 8)]
        return jnp.concatenate(merged, axis=0)

    @pl.loop(0, bins, unroll=16)
    def _(index):
        rows = pl.ds(index, every, stride=PITCH)
        first = first_rows[rows, :]
        second = second_rows[rows, :]
        turned = pltpu.roll(second, half, axis=1)
        real_x = jnp.where(left, first, turned)
        imag_x = jnp.where(left, pltpu.roll(first, half, axis=1), second)
        partner = jnp.concatenate([real_x, imag_x], axis=0).T.astype(BF16)
        own = jnp.concatenate(
            [
                jnp.concatenate([real_x, imag_x], axis=1),
                jnp.concatenate([imag_x, -real_x], axis=1),
            ],
            axis=0,
        ).astype(BF16)
        gram = jnp.dot(partner, own, preferred_element_type=F32)
        for part in range(2):
            value = skewed(gram[:, part * LANES : (part + 1) * LANES]) * keep
            part_ref[pl.ds(index, 1), part] = value[None]
        late = jnp.concatenate([second, jnp.where(left, turned, -turned)], axis=0)
        later_ref[pl.ds(index, 1)] = late.astype(BF16)[None]


def next_kernel(limit_ref, part_ref, later_ref, next_ref, out_ref, next_all, held, sent):
    groups, windows, _, _ = next_ref.shape
    steps, bins = held.shape[0], held.shape[3]
    every = groups * windows
    half = LANES // 2
    lane = lax.broadcasted_iota(jnp.int32, (half, LANES), 1)
    back = half - 1 - (lane & (half - 1))
    row = lax.broadcasted_iota(jnp.int32, (8, LANES), 0)
    spot = row - (back[:8] & 7)

    def lowered(gram):
        for bit in (32, 16, 8):
            moved = jnp.concatenate([jnp.zeros((bit, LANES), F32), gram[: half - bit]], axis=0)
            gram = jnp.where((back & bit) != 0, moved, gram)
        pieces = [jnp.zeros((8, LANES), F32)] + [
            jnp.take_along_axis(gram[at : at + 8], spot & 7, axis=0) for at in range(0, half, 8)
        ]
        merged = [jnp.where(spot >= 0, pieces[p + 1], pieces[p]) for p in range(half // 8)]
        return jnp.concatenate(merged, axis=0)

    offsets = lax.broadcasted_iota(jnp.int32, (OFFSETS, LANES), 0) + 1
    lanes = lax.broadcasted_iota(jnp.int32, (OFFSETS, LANES), 1)
    keep = ((offsets <= limit_ref[...]) & (lanes >= half)).astype(F32)

    def send(step):
        where = pl.ds(pl.multiple_of(step * bins, bins), bins)
        return pltpu.make_async_copy(held.at[step], out_ref.at[:, :, where], sent.at[step])

    @pl.loop(0, steps)
    def _(step):
        base = pl.multiple_of(step * bins, bins)
        after_all = next_ref[:, :, pl.ds(base, bins)]
        next_all[:, :bins] = after_all.astype(F32).reshape(every, bins, LANES)
        next_rows = next_all.reshape(every * PITCH, LANES)

        def next_part(index):
            after = next_rows[pl.ds(index, every, stride=PITCH), :]
            partner = jnp.concatenate([after, pltpu.roll(after, half, axis=1)], axis=0)
            partner = partner.T[:half].astype(BF16)
            return lowered(jnp.dot(partner, later_ref[base + index], preferred_element_type=F32))

        for start in range(0, bins, 8):
            extra = [next_part(start + at) for at in range(8)]
            for part in range(2):
                for tile in range(0, OFFSETS, 8):
                    sums = []
                    for at in range(8):
                        value = extra[at][tile : tile + 8]
                        if part == 0:
                            value = pltpu.roll(value, half, axis=1)
                        value = value * keep[tile : tile + 8]
                        own = part_ref[base + start + at, part, tile : tile + 8]
                        sums.append(own + value)
                    for at, value in enumerate(swapped(sums)):
                        held[step, tile + at, part, start : start + 8] = value
        send(step).start()

    for step in range(steps):
        send(step).wait()


def own_spectra(limit, halves):
    groups, _, windows, bins, _ = halves.shape
    step = 16
    every = groups * windows
    scratch = pltpu.VMEM((every, PITCH, LANES), F32)
    return pl.pallas_call(
        own_kernel,
        grid=(bins // step,),
        in_specs=[
            pl.BlockSpec((1, LANES), lambda b: (0, 0)),
            pl.BlockSpec((groups, 2, windows, step, LANES), lambda b: (0, 0, 0, b, 0)),
        ],
        out_specs=[
            pl.BlockSpec((step, 2, OFFSETS, LANES), lambda b: (b, 0, 0, 0)),
            pl.BlockSpec((step, 2 * every, LANES), lambda b: (b, 0, 0)),
        ],
        out_shape=[
            jax.ShapeDtypeStruct((bins, 2, OFFSETS, LANES), F32),
            jax.ShapeDtypeStruct((bins, 2 * every, LANES), BF16),
        ],
        scratch_shapes=[scratch] * 2,
        compiler_params=pltpu.CompilerParams(vmem_limit_bytes=20 * 2**20),
        cost_estimate=pl.CostEstimate(
            flops=2 * bins * 128 * 96 * 256,
            bytes_accessed=4 * halves.size + 4 * OFFSETS * 2 * bins * LANES,
            transcendentals=0,
        ),
        name="own_spectra",
    )(limit, halves)


def next_spectra(limit, own, later, after):
    groups, windows, bins, _ = after.shape
    step = 16
    every = groups * windows
    resident = pl.BlockSpec(memory_space=pltpu.VMEM)
    return pl.pallas_call(
        next_kernel,
        in_specs=[resident] * 4,
        out_specs=pl.BlockSpec(memory_space=pl.ANY),
        out_shape=jax.ShapeDtypeStruct((OFFSETS, 2, bins, LANES), F32),
        scratch_shapes=[
            pltpu.VMEM((every, PITCH, LANES), F32),
            pltpu.VMEM((bins // step, OFFSETS, 2, step, LANES), F32),
            pltpu.SemaphoreType.DMA((bins // step,)),
        ],
        compiler_params=pltpu.CompilerParams(vmem_limit_bytes=20 * 2**20),
        cost_estimate=pl.CostEstimate(
            flops=2 * bins * 64 * 96 * 128,
            bytes_accessed=2 * after.size + 8 * OFFSETS * 2 * bins * LANES,
            transcendentals=0,
        ),
        name="next_spectra",
    )(limit, own, later, after)


def exchanged(blocks, axis):
    flat = blocks.reshape(blocks.shape[0], -1, LANES)
    flat = lax.all_to_all(flat, axis, split_axis=0, concat_axis=0, tiled=True)
    return flat.reshape(blocks.shape)


def body(down, back, records, channel_live, offset_limit):
    parts = lax.axis_size("fibre")
    groups = lax.axis_size("freq")
    sums = project(down, records, parts)
    sums = exchanged(sums, "fibre")
    halves = whiten(channel_live[None, :], back, sums, groups)
    halves = exchanged(halves, "freq")
    after = lax.ppermute(halves[:, 0], "fibre", [(i, i - 1) for i in range(1, parts)])
    own, later = own_spectra(offset_limit[None, :], halves)
    return next_spectra(offset_limit[None, :], own, later, after)


def solution(mesh):
    down, back = make_tables(mesh.shape["fibre"])
    down = np.concatenate(split_pair(down))
    back = split_pair(back)[0]
    return jax.shard_map(
        functools.partial(body, down, back),
        mesh=mesh,
        in_specs=(P("freq", "fibre", None), P("fibre"), P("fibre")),
        out_specs=P(None, None, "freq", "fibre"),
        check_vma=False,
    )
```

```python
import functools

import jax
import jax.numpy as jnp
import numpy as np
from jax import lax
from jax.experimental import pallas as pl
from jax.experimental.pallas import tpu as pltpu
from jax.sharding import PartitionSpec as P

SAMPLES = 6000
NB = 512
HALF = 32
FIRST_BIN = 60
OFFSETS = 64
BINS = NB + 2 * HALF
RANK = 96
PITCH = 24
LANES = 128
F32 = jnp.float32
BF16 = jnp.bfloat16


def split_pair(values):
    high = values.astype(jnp.bfloat16)
    low = (values - high.astype(np.float64)).astype(jnp.bfloat16)
    return high, low


def make_tables(parts):
    run = SAMPLES // parts
    times = np.arange(run) - (run - 1) / 2
    bins = np.arange(FIRST_BIN - 1, FIRST_BIN + BINS + 1)
    weight = 1.0 + np.arange(len(bins)) / len(bins)
    angles = 2.0 * np.pi * np.outer(times, bins) / SAMPLES
    rows = []
    for wave in (np.cos, np.sin):
        vectors = np.linalg.svd(wave(angles) * weight, full_matrices=False)[0]
        vectors = vectors[:, : RANK // 2]
        rows.append((vectors * np.sign(vectors[run // 2 + 3])).T)
    down = np.concatenate(rows)
    samples = np.arange(SAMPLES)
    kept = np.arange(FIRST_BIN, FIRST_BIN + BINS)
    taper = 0.5 - 0.5 * np.cos(2.0 * np.pi * samples / SAMPLES)
    phase = 2.0 * np.pi * (np.outer(samples, kept) % SAMPLES) / SAMPLES
    table = np.concatenate([np.cos(phase), -np.sin(phase)], axis=1) * taper[:, None]
    back = np.einsum("psj,rs->jpr", table.reshape(parts, run, 2 * BINS), down)
    return down, back.reshape(2 * BINS, parts * RANK)


def project_kernel(down_ref, records_ref, out_ref, held, table, arrived):
    parts, windows = out_ref.shape[:2]
    wide = 4

    def fetch(window):
        return pltpu.make_async_copy(records_ref.at[window], held.at[window], arrived.at[window])

    fetch_table = pltpu.make_async_copy(down_ref, table, arrived.at[windows])
    fetch_table.start()
    for window in range(windows):
        fetch(window).start()
    fetch_table.wait()
    for window in range(windows):
        fetch(window).wait()
        for start in range(0, parts, wide):
            block = held[window, :, start * LANES : (start + wide) * LANES]
            both = jnp.dot(table[...], block, preferred_element_type=F32)
            sums = (both[:RANK] + both[RANK:]).astype(BF16)
            for part in range(wide):
                out_ref[start + part, window] = sums[:, part * LANES : (part + 1) * LANES]


def project(down, records, parts):
    windows, run, channels = records.shape
    down = pltpu.with_memory_space_constraint(down, pltpu.HBM)
    records = pltpu.with_memory_space_constraint(records, pltpu.HBM)
    return pl.pallas_call(
        project_kernel,
        in_specs=[pl.BlockSpec(memory_space=pltpu.HBM)] * 2,
        out_specs=pl.BlockSpec(memory_space=pltpu.VMEM),
        out_shape=jax.ShapeDtypeStruct((parts, windows, RANK, LANES), BF16),
        scratch_shapes=[
            pltpu.VMEM(records.shape, BF16),
            pltpu.VMEM(down.shape, BF16),
            pltpu.SemaphoreType.DMA((windows + 1,)),
        ],
        compiler_params=pltpu.CompilerParams(vmem_limit_bytes=24 * 2**20),
        cost_estimate=pl.CostEstimate(
            flops=4 * RANK * run * channels * windows,
            bytes_accessed=2 * records.size + 2 * parts * windows * RANK * LANES,
            transcendentals=0,
        ),
        name="project",
    )(down, records)


def up_by(values, rows):
    return pltpu.roll(values, values.shape[0] - rows, axis=0)


def whiten_kernel(live_ref, back_ref, sums_ref, out_ref, spectra):
    parts, windows = sums_ref.shape[:2]
    groups = out_ref.shape[0]
    rows = 2 * BINS // 3
    live = live_ref[...].astype(F32)
    live = jnp.concatenate([live, live], axis=1)
    left = lax.broadcasted_iota(jnp.int32, (NB, LANES), 1) < LANES // 2

    def transform(pair):
        columns = jnp.concatenate(
            [sums_ref[:, 2 * pair + i].reshape(parts * RANK, LANES) for i in range(2)], axis=1
        )
        for start in range(0, 2 * BINS, rows):
            spectra[pair % 2, start : start + rows] = jnp.dot(
                back_ref[start : start + rows], columns, preferred_element_type=F32
            )

    transform(0)
    for pair in range(windows // 2):
        if 2 * pair + 2 < windows:
            transform(pair + 1)
        real_part = spectra[pair % 2, :BINS]
        imag_part = spectra[pair % 2, BINS:]
        amplitude = jnp.sqrt(real_part * real_part + imag_part * imag_part)
        total = amplitude
        for reach in (8, 16, 32):
            total = total[: total.shape[0] - reach] + total[reach:]
        for reach in (1, 2, 4):
            total = total + up_by(total, reach)
        smooth = (total[:NB] + amplitude[2 * HALF :]) * (1.0 / (2 * HALF + 1))
        scale = live / (smooth + 1e-06)
        real_part = real_part[HALF : HALF + NB] * scale
        imag_part = imag_part[HALF : HALF + NB] * scale
        for i in range(2):
            real_one = real_part[:, i * LANES : (i + 1) * LANES]
            imag_one = imag_part[:, i * LANES : (i + 1) * LANES]
            first = jnp.where(left, real_one, pltpu.roll(imag_one, LANES // 2, axis=1))
            second = jnp.where(left, pltpu.roll(real_one, LANES // 2, axis=1), imag_one)
            for half, value in enumerate((first, second)):
                value = value.astype(BF16).reshape(groups, NB // groups, LANES)
                out_ref[:, half, 2 * pair + i] = value


def whiten(live, back, sums, groups):
    parts, windows = sums.shape[:2]
    resident = pl.BlockSpec(memory_space=pltpu.VMEM)
    return pl.pallas_call(
        whiten_kernel,
        in_specs=[resident] * 3,
        out_specs=resident,
        out_shape=jax.ShapeDtypeStruct((groups, 2, windows, NB // groups, LANES), BF16),
        scratch_shapes=[pltpu.VMEM((2, 2 * BINS, 2 * LANES), F32)],
        compiler_params=pltpu.CompilerParams(vmem_limit_bytes=28 * 2**20),
        cost_estimate=pl.CostEstimate(
            flops=2 * back.size * windows * LANES,
            bytes_accessed=2 * (back.size + sums.size + 2 * windows * NB * LANES),
            transcendentals=0,
        ),
        name="whiten",
    )(live, back, sums)


def swapped(tiles):
    row = lax.broadcasted_iota(jnp.int32, (8, LANES), 0)
    moved = [tiles[0]] + [pltpu.roll(tiles[j], j, axis=0) for j in range(1, 8)]
    for bit in (1, 2, 4):
        take = (row & bit) != 0
        moved = [jnp.where(take, moved[(j + bit) % 8], moved[j]) for j in range(8)]
    return [moved[0]] + [pltpu.roll(moved[8 - i], 8 - i, axis=0) for i in range(1, 8)]


def own_kernel(limit_ref, halves_ref, part_ref, later_ref, first_all, second_all):
    groups, _, windows, bins, _ = halves_ref.shape
    every = groups * windows
    half = LANES // 2
    first_all[:, :bins] = halves_ref[:, 0].astype(F32).reshape(every, bins, LANES)
    second_all[:, :bins] = halves_ref[:, 1].astype(F32).reshape(every, bins, LANES)
    first_rows = first_all.reshape(every * PITCH, LANES)
    second_rows = second_all.reshape(every * PITCH, LANES)
    left = lax.broadcasted_iota(jnp.int32, (every, LANES), 1) < half
    offsets = lax.broadcasted_iota(jnp.int32, (OFFSETS, LANES), 0) + 1
    keep = (offsets <= limit_ref[...]).astype(F32)
    lane = lax.broadcasted_iota(jnp.int32, (LANES, LANES), 1)
    turn = (lane[:8] & 7) + 1
    spot = lax.broadcasted_iota(jnp.int32, (8, LANES), 0) + turn

    def skewed(gram):
        gram = jnp.concatenate([gram, jnp.zeros((OFFSETS, LANES), F32)], axis=0)
        for bit in (64, 32, 16, 8):
            rows = min(gram.shape[0] - bit, LANES)
            gram = jnp.where((lane[:rows] & bit) != 0, gram[bit : bit + rows], gram[:rows])
        pieces = [
            jnp.take_along_axis(gram[row : row + 8], spot & 7, axis=0)
            for row in range(0, OFFSETS + 8, 8)
        ]
        merged = [jnp.where(spot < 8, pieces[p], pieces[p + 1]) for p in range(OFFSETS // 8)]
        return jnp.concatenate(merged, axis=0)

    @pl.loop(0, bins, unroll=16)
    def _(index):
        rows = pl.ds(index, every, stride=PITCH)
        first = first_rows[rows, :]
        second = second_rows[rows, :]
        turned = pltpu.roll(second, half, axis=1)
        real_x = jnp.where(left, first, turned)
        imag_x = jnp.where(left, pltpu.roll(first, half, axis=1), second)
        partner = jnp.concatenate([real_x, imag_x], axis=0).T.astype(BF16)
        own = jnp.concatenate(
            [
                jnp.concatenate([real_x, imag_x], axis=1),
                jnp.concatenate([imag_x, -real_x], axis=1),
            ],
            axis=0,
        ).astype(BF16)
        gram = jnp.dot(partner, own, preferred_element_type=F32)
        for part in range(2):
            value = skewed(gram[:, part * LANES : (part + 1) * LANES]) * keep
            part_ref[pl.ds(index, 1), part] = value[None]
        late = jnp.concatenate([second, jnp.where(left, turned, -turned)], axis=0)
        later_ref[pl.ds(index, 1)] = late.astype(BF16)[None]


def next_kernel(limit_ref, part_ref, later_ref, next_ref, out_ref, next_all, held, sent):
    groups, windows, _, _ = next_ref.shape
    steps, bins = held.shape[0], held.shape[3]
    every = groups * windows
    half = LANES // 2
    lane = lax.broadcasted_iota(jnp.int32, (half, LANES), 1)
    back = half - 1 - (lane & (half - 1))
    row = lax.broadcasted_iota(jnp.int32, (8, LANES), 0)
    spot = row - (back[:8] & 7)

    def lowered(gram):
        for bit in (32, 16, 8):
            moved = jnp.concatenate([jnp.zeros((bit, LANES), F32), gram[: half - bit]], axis=0)
            gram = jnp.where((back & bit) != 0, moved, gram)
        pieces = [jnp.zeros((8, LANES), F32)] + [
            jnp.take_along_axis(gram[at : at + 8], spot & 7, axis=0) for at in range(0, half, 8)
        ]
        merged = [jnp.where(spot >= 0, pieces[p + 1], pieces[p]) for p in range(half // 8)]
        return jnp.concatenate(merged, axis=0)

    offsets = lax.broadcasted_iota(jnp.int32, (OFFSETS, LANES), 0) + 1
    lanes = lax.broadcasted_iota(jnp.int32, (OFFSETS, LANES), 1)
    keep = ((offsets <= limit_ref[...]) & (lanes >= half)).astype(F32)

    def send(step):
        where = pl.ds(pl.multiple_of(step * bins, bins), bins)
        return pltpu.make_async_copy(held.at[step], out_ref.at[:, :, where], sent.at[step])

    @pl.loop(0, steps)
    def _(step):
        base = pl.multiple_of(step * bins, bins)
        after_all = next_ref[:, :, pl.ds(base, bins)]
        next_all[:, :bins] = after_all.astype(F32).reshape(every, bins, LANES)
        next_rows = next_all.reshape(every * PITCH, LANES)

        def next_part(index):
            after = next_rows[pl.ds(index, every, stride=PITCH), :]
            partner = after.astype(BF16).T
            later = later_ref[base + index]
            gram = jnp.dot(partner[:half], later[:every], preferred_element_type=F32)
            gram += jnp.dot(partner[half:], later[every:], preferred_element_type=F32)
            return lowered(gram)

        for start in range(0, bins, 8):
            extra = [next_part(start + at) for at in range(8)]
            for part in range(2):
                for tile in range(0, OFFSETS, 8):
                    sums = []
                    for at in range(8):
                        value = extra[at][tile : tile + 8]
                        if part == 0:
                            value = pltpu.roll(value, half, axis=1)
                        value = value * keep[tile : tile + 8]
                        own = part_ref[base + start + at, part, tile : tile + 8]
                        sums.append(own + value)
                    for at, value in enumerate(swapped(sums)):
                        held[step, tile + at, part, start : start + 8] = value
        send(step).start()

    for step in range(steps):
        send(step).wait()


def own_spectra(limit, halves):
    groups, _, windows, bins, _ = halves.shape
    step = 16
    every = groups * windows
    scratch = pltpu.VMEM((every, PITCH, LANES), F32)
    return pl.pallas_call(
        own_kernel,
        grid=(bins // step,),
        in_specs=[
            pl.BlockSpec((1, LANES), lambda b: (0, 0)),
            pl.BlockSpec((groups, 2, windows, step, LANES), lambda b: (0, 0, 0, b, 0)),
        ],
        out_specs=[
            pl.BlockSpec((step, 2, OFFSETS, LANES), lambda b: (b, 0, 0, 0)),
            pl.BlockSpec((step, 2 * every, LANES), lambda b: (b, 0, 0)),
        ],
        out_shape=[
            jax.ShapeDtypeStruct((bins, 2, OFFSETS, LANES), F32),
            jax.ShapeDtypeStruct((bins, 2 * every, LANES), BF16),
        ],
        scratch_shapes=[scratch] * 2,
        compiler_params=pltpu.CompilerParams(vmem_limit_bytes=20 * 2**20),
        cost_estimate=pl.CostEstimate(
            flops=2 * bins * 128 * 96 * 256,
            bytes_accessed=4 * halves.size + 4 * OFFSETS * 2 * bins * LANES,
            transcendentals=0,
        ),
        name="own_spectra",
    )(limit, halves)


def next_spectra(limit, own, later, after):
    groups, windows, bins, _ = after.shape
    step = 16
    every = groups * windows
    resident = pl.BlockSpec(memory_space=pltpu.VMEM)
    return pl.pallas_call(
        next_kernel,
        in_specs=[resident] * 4,
        out_specs=pl.BlockSpec(memory_space=pl.ANY),
        out_shape=jax.ShapeDtypeStruct((OFFSETS, 2, bins, LANES), F32),
        scratch_shapes=[
            pltpu.VMEM((every, PITCH, LANES), F32),
            pltpu.VMEM((bins // step, OFFSETS, 2, step, LANES), F32),
            pltpu.SemaphoreType.DMA((bins // step,)),
        ],
        compiler_params=pltpu.CompilerParams(vmem_limit_bytes=20 * 2**20),
        cost_estimate=pl.CostEstimate(
            flops=2 * bins * 64 * 96 * 128,
            bytes_accessed=2 * after.size + 8 * OFFSETS * 2 * bins * LANES,
            transcendentals=0,
        ),
        name="next_spectra",
    )(limit, own, later, after)


def exchanged(blocks, axis):
    flat = blocks.reshape(blocks.shape[0], -1, LANES)
    flat = lax.all_to_all(flat, axis, split_axis=0, concat_axis=0, tiled=True)
    return flat.reshape(blocks.shape)


def body(down, back, records, channel_live, offset_limit):
    parts = lax.axis_size("fibre")
    groups = lax.axis_size("freq")
    sums = project(down, records, parts)
    sums = exchanged(sums, "fibre")
    halves = whiten(channel_live[None, :], back, sums, groups)
    halves = exchanged(halves, "freq")
    after = lax.ppermute(halves[:, 0], "fibre", [(i, i - 1) for i in range(1, parts)])
    own, later = own_spectra(offset_limit[None, :], halves)
    return next_spectra(offset_limit[None, :], own, later, after)


def solution(mesh):
    down, back = make_tables(mesh.shape["fibre"])
    down = np.concatenate(split_pair(down))
    back = split_pair(back)[0]
    return jax.shard_map(
        functools.partial(body, down, back),
        mesh=mesh,
        in_specs=(P("freq", "fibre", None), P("fibre"), P("fibre")),
        out_specs=P(None, None, "freq", "fibre"),
        check_vma=False,
    )
```

```python
import functools

import jax
import jax.numpy as jnp
import numpy as np
from jax import lax
from jax.experimental import pallas as pl
from jax.experimental.pallas import tpu as pltpu
from jax.sharding import PartitionSpec as P

SAMPLES = 6000
NB = 512
HALF = 32
FIRST_BIN = 60
OFFSETS = 64
BINS = NB + 2 * HALF
RANK = 96
PITCH = 24
LANES = 128
F32 = jnp.float32
BF16 = jnp.bfloat16


def split_pair(values):
    high = values.astype(jnp.bfloat16)
    low = (values - high.astype(np.float64)).astype(jnp.bfloat16)
    return high, low


def make_tables(parts):
    run = SAMPLES // parts
    times = np.arange(run) - (run - 1) / 2
    bins = np.arange(FIRST_BIN - 1, FIRST_BIN + BINS + 1)
    weight = 1.0 + np.arange(len(bins)) / len(bins)
    angles = 2.0 * np.pi * np.outer(times, bins) / SAMPLES
    rows = []
    for wave in (np.cos, np.sin):
        vectors = np.linalg.svd(wave(angles) * weight, full_matrices=False)[0]
        vectors = vectors[:, : RANK // 2]
        rows.append((vectors * np.sign(vectors[run // 2 + 3])).T)
    down = np.concatenate(rows)
    samples = np.arange(SAMPLES)
    kept = np.arange(FIRST_BIN, FIRST_BIN + BINS)
    taper = 0.5 - 0.5 * np.cos(2.0 * np.pi * samples / SAMPLES)
    phase = 2.0 * np.pi * (np.outer(samples, kept) % SAMPLES) / SAMPLES
    table = np.concatenate([np.cos(phase), -np.sin(phase)], axis=1) * taper[:, None]
    back = np.einsum("psj,rs->jpr", table.reshape(parts, run, 2 * BINS), down)
    return down, back.reshape(2 * BINS, parts * RANK)


def project_kernel(down_ref, records_ref, out_ref, held, table, arrived):
    parts, windows = out_ref.shape[:2]
    wide = 4

    def fetch(window):
        return pltpu.make_async_copy(records_ref.at[window], held.at[window], arrived.at[window])

    fetch_table = pltpu.make_async_copy(down_ref, table, arrived.at[windows])
    fetch_table.start()
    for window in range(windows):
        fetch(window).start()
    fetch_table.wait()
    for window in range(windows):
        fetch(window).wait()
        for start in range(0, parts, wide):
            block = held[window, :, start * LANES : (start + wide) * LANES]
            both = jnp.dot(table[...], block, preferred_element_type=F32)
            sums = (both[:RANK] + both[RANK:]).astype(BF16)
            for part in range(wide):
                out_ref[start + part, window] = sums[:, part * LANES : (part + 1) * LANES]


def project(down, records, parts):
    windows, run, channels = records.shape
    down = pltpu.with_memory_space_constraint(down, pltpu.HBM)
    records = pltpu.with_memory_space_constraint(records, pltpu.HBM)
    return pl.pallas_call(
        project_kernel,
        in_specs=[pl.BlockSpec(memory_space=pltpu.HBM)] * 2,
        out_specs=pl.BlockSpec(memory_space=pltpu.VMEM),
        out_shape=jax.ShapeDtypeStruct((parts, windows, RANK, LANES), BF16),
        scratch_shapes=[
            pltpu.VMEM(records.shape, BF16),
            pltpu.VMEM(down.shape, BF16),
            pltpu.SemaphoreType.DMA((windows + 1,)),
        ],
        compiler_params=pltpu.CompilerParams(vmem_limit_bytes=24 * 2**20),
        cost_estimate=pl.CostEstimate(
            flops=4 * RANK * run * channels * windows,
            bytes_accessed=2 * records.size + 2 * parts * windows * RANK * LANES,
            transcendentals=0,
        ),
        name="project",
    )(down, records)


def up_by(values, rows):
    return pltpu.roll(values, values.shape[0] - rows, axis=0)


def whiten_kernel(live_ref, back_ref, sums_ref, out_ref, spectra):
    parts, windows = sums_ref.shape[:2]
    groups = out_ref.shape[0]
    rows = 2 * BINS // 3
    live = live_ref[...].astype(F32)
    live = jnp.concatenate([live, live], axis=1)
    left = lax.broadcasted_iota(jnp.int32, (NB, LANES), 1) < LANES // 2

    def transform(pair):
        columns = jnp.concatenate(
            [sums_ref[:, 2 * pair + i].reshape(parts * RANK, LANES) for i in range(2)], axis=1
        )
        for start in range(0, 2 * BINS, rows):
            spectra[pair % 2, start : start + rows] = jnp.dot(
                back_ref[start : start + rows], columns, preferred_element_type=F32
            )

    transform(0)
    for pair in range(windows // 2):
        if 2 * pair + 2 < windows:
            transform(pair + 1)
        real_part = spectra[pair % 2, :BINS]
        imag_part = spectra[pair % 2, BINS:]
        amplitude = jnp.sqrt(real_part * real_part + imag_part * imag_part)
        total = amplitude
        for reach in (8, 16, 32):
            total = total[: total.shape[0] - reach] + total[reach:]
        for reach in (1, 2, 4):
            total = total + up_by(total, reach)
        smooth = (total[:NB] + amplitude[2 * HALF :]) * (1.0 / (2 * HALF + 1))
        scale = live / (smooth + 1e-06)
        real_part = real_part[HALF : HALF + NB] * scale
        imag_part = imag_part[HALF : HALF + NB] * scale
        for i in range(2):
            real_one = real_part[:, i * LANES : (i + 1) * LANES]
            imag_one = imag_part[:, i * LANES : (i + 1) * LANES]
            first = jnp.where(left, real_one, pltpu.roll(imag_one, LANES // 2, axis=1))
            second = jnp.where(left, pltpu.roll(real_one, LANES // 2, axis=1), imag_one)
            for half, value in enumerate((first, second)):
                value = value.astype(BF16).reshape(groups, NB // groups, LANES)
                out_ref[:, half, 2 * pair + i] = value


def whiten(live, back, sums, groups):
    parts, windows = sums.shape[:2]
    resident = pl.BlockSpec(memory_space=pltpu.VMEM)
    return pl.pallas_call(
        whiten_kernel,
        in_specs=[resident] * 3,
        out_specs=resident,
        out_shape=jax.ShapeDtypeStruct((groups, 2, windows, NB // groups, LANES), BF16),
        scratch_shapes=[pltpu.VMEM((2, 2 * BINS, 2 * LANES), F32)],
        compiler_params=pltpu.CompilerParams(vmem_limit_bytes=28 * 2**20),
        cost_estimate=pl.CostEstimate(
            flops=2 * back.size * windows * LANES,
            bytes_accessed=2 * (back.size + sums.size + 2 * windows * NB * LANES),
            transcendentals=0,
        ),
        name="whiten",
    )(live, back, sums)


def swapped(tiles):
    row = lax.broadcasted_iota(jnp.int32, (8, LANES), 0)
    moved = [tiles[0]] + [pltpu.roll(tiles[j], j, axis=0) for j in range(1, 8)]
    for bit in (1, 2, 4):
        take = (row & bit) != 0
        moved = [jnp.where(take, moved[(j + bit) % 8], moved[j]) for j in range(8)]
    return [moved[0]] + [pltpu.roll(moved[8 - i], 8 - i, axis=0) for i in range(1, 8)]


def own_kernel(limit_ref, halves_ref, part_ref, later_ref, first_all, second_all):
    groups, _, windows, bins, _ = halves_ref.shape
    every = groups * windows
    half = LANES // 2
    first_all[:, :bins] = halves_ref[:, 0].astype(F32).reshape(every, bins, LANES)
    second_all[:, :bins] = halves_ref[:, 1].astype(F32).reshape(every, bins, LANES)
    first_rows = first_all.reshape(every * PITCH, LANES)
    second_rows = second_all.reshape(every * PITCH, LANES)
    left = lax.broadcasted_iota(jnp.int32, (every, LANES), 1) < half
    offsets = lax.broadcasted_iota(jnp.int32, (OFFSETS, LANES), 0) + 1
    keep = (offsets <= limit_ref[...]).astype(F32)
    lane = lax.broadcasted_iota(jnp.int32, (LANES, LANES), 1)
    turn = (lane[:8] & 7) + 1
    spot = lax.broadcasted_iota(jnp.int32, (8, LANES), 0) + turn

    def skewed(gram):
        gram = jnp.concatenate([gram, jnp.zeros((OFFSETS, LANES), F32)], axis=0)
        for bit in (64, 32, 16, 8):
            rows = min(gram.shape[0] - bit, LANES)
            gram = jnp.where((lane[:rows] & bit) != 0, gram[bit : bit + rows], gram[:rows])
        pieces = [
            jnp.take_along_axis(gram[row : row + 8], spot & 7, axis=0)
            for row in range(0, OFFSETS + 8, 8)
        ]
        merged = [jnp.where(spot < 8, pieces[p], pieces[p + 1]) for p in range(OFFSETS // 8)]
        return jnp.concatenate(merged, axis=0)

    @pl.loop(0, bins, unroll=16)
    def _(index):
        rows = pl.ds(index, every, stride=PITCH)
        first = first_rows[rows, :]
        second = second_rows[rows, :]
        turned = pltpu.roll(second, half, axis=1)
        real_x = jnp.where(left, first, turned)
        imag_x = jnp.where(left, pltpu.roll(first, half, axis=1), second)
        partner = jnp.concatenate([real_x, imag_x], axis=0).T.astype(BF16)
        own = jnp.concatenate(
            [
                jnp.concatenate([real_x, imag_x], axis=1),
                jnp.concatenate([imag_x, -real_x], axis=1),
            ],
            axis=0,
        ).astype(BF16)
        gram = jnp.dot(partner, own, preferred_element_type=F32)
        for part in range(2):
            value = skewed(gram[:, part * LANES : (part + 1) * LANES]) * keep
            part_ref[pl.ds(index, 1), part] = value[None]
        late = jnp.concatenate([second, jnp.where(left, turned, -turned)], axis=0)
        later_ref[pl.ds(index, 1)] = late.astype(BF16)[None]


def next_kernel(begin, limit_ref, part_ref, later_ref, next_ref, *refs):
    out_ref, next_all, held, sent = refs[-4:]
    groups, windows, _, _ = next_ref.shape
    steps, bins = held.shape[0] // 2, 16
    every = groups * windows
    half = LANES // 2
    lane = lax.broadcasted_iota(jnp.int32, (half, LANES), 1)
    back = half - 1 - (lane & (half - 1))
    row = lax.broadcasted_iota(jnp.int32, (8, LANES), 0)
    spot = row - (back[:8] & 7)

    def lowered(gram):
        for bit in (32, 16, 8):
            moved = jnp.concatenate([jnp.zeros((bit, LANES), F32), gram[: half - bit]], axis=0)
            gram = jnp.where((back & bit) != 0, moved, gram)
        pieces = [jnp.zeros((8, LANES), F32)] + [
            jnp.take_along_axis(gram[at : at + 8], spot & 7, axis=0) for at in range(0, half, 8)
        ]
        merged = [jnp.where(spot >= 0, pieces[p + 1], pieces[p]) for p in range(half // 8)]
        return jnp.concatenate(merged, axis=0)

    offsets = lax.broadcasted_iota(jnp.int32, (OFFSETS, LANES), 0) + 1
    lanes = lax.broadcasted_iota(jnp.int32, (OFFSETS, LANES), 1)
    keep = ((offsets <= limit_ref[...]) & (lanes >= half)).astype(F32)

    def send(step):
        where = pl.ds(pl.multiple_of(begin + step * 8, 8), 8)
        return pltpu.make_async_copy(held.at[step], out_ref.at[:, :, where], sent.at[step])

    @pl.loop(0, steps)
    def _(step):
        base = begin + step * bins
        after_all = next_ref[:, :, pl.ds(pl.multiple_of(step * bins, bins), bins)]
        next_all[:, :bins] = after_all.astype(F32).reshape(every, bins, LANES)
        next_rows = next_all.reshape(every * PITCH, LANES)

        def next_part(index):
            after = next_rows[pl.ds(index, every, stride=PITCH), :]
            partner = after.astype(BF16).T
            later = later_ref[base + index]
            gram = jnp.dot(partner[:half], later[:every], preferred_element_type=F32)
            gram += jnp.dot(partner[half:], later[every:], preferred_element_type=F32)
            return lowered(gram)

        for start in range(0, bins, 8):
            extra = [next_part(start + at) for at in range(8)]
            for part in range(2):
                for tile in range(0, OFFSETS, 8):
                    sums = []
                    for at in range(8):
                        value = extra[at][tile : tile + 8]
                        if part == 0:
                            value = pltpu.roll(value, half, axis=1)
                        value = value * keep[tile : tile + 8]
                        own = part_ref[base + start + at, part, tile : tile + 8]
                        sums.append(own + value)
                    for at, value in enumerate(swapped(sums)):
                        held[2 * step + start // 8, tile + at, part] = value
            send(2 * step + start // 8).start()

    for step in range(2 * steps):
        send(step).wait()


def own_spectra(limit, halves):
    groups, _, windows, bins, _ = halves.shape
    step = 16
    every = groups * windows
    scratch = pltpu.VMEM((every, PITCH, LANES), F32)
    return pl.pallas_call(
        own_kernel,
        grid=(bins // step,),
        in_specs=[
            pl.BlockSpec((1, LANES), lambda b: (0, 0)),
            pl.BlockSpec((groups, 2, windows, step, LANES), lambda b: (0, 0, 0, b, 0)),
        ],
        out_specs=[
            pl.BlockSpec((step, 2, OFFSETS, LANES), lambda b: (b, 0, 0, 0)),
            pl.BlockSpec((step, 2 * every, LANES), lambda b: (b, 0, 0)),
        ],
        out_shape=[
            jax.ShapeDtypeStruct((bins, 2, OFFSETS, LANES), F32),
            jax.ShapeDtypeStruct((bins, 2 * every, LANES), BF16),
        ],
        scratch_shapes=[scratch] * 2,
        compiler_params=pltpu.CompilerParams(vmem_limit_bytes=20 * 2**20),
        cost_estimate=pl.CostEstimate(
            flops=2 * bins * 128 * 96 * 256,
            bytes_accessed=4 * halves.size + 4 * OFFSETS * 2 * bins * LANES,
            transcendentals=0,
        ),
        name="own_spectra",
    )(limit, halves)


def next_spectra(limit, own, later, after, begin, done):
    groups, windows, bins, _ = after.shape
    step = 16
    every = groups * windows
    resident = pl.BlockSpec(memory_space=pltpu.VMEM)
    anywhere = pl.BlockSpec(memory_space=pl.ANY)
    filled = [] if done is None else [done]
    return pl.pallas_call(
        functools.partial(next_kernel, begin),
        in_specs=[resident] * 4 + [anywhere] * len(filled),
        out_specs=anywhere,
        out_shape=jax.ShapeDtypeStruct((OFFSETS, 2, own.shape[0], LANES), F32),
        input_output_aliases={4: 0} if filled else {},
        scratch_shapes=[
            pltpu.VMEM((every, PITCH, LANES), F32),
            pltpu.VMEM((bins // 8, OFFSETS, 2, 8, LANES), F32),
            pltpu.SemaphoreType.DMA((bins // 8,)),
        ],
        compiler_params=pltpu.CompilerParams(vmem_limit_bytes=20 * 2**20),
        cost_estimate=pl.CostEstimate(
            flops=2 * bins * 64 * 96 * 128,
            bytes_accessed=2 * after.size + 8 * OFFSETS * 2 * bins * LANES,
            transcendentals=0,
        ),
        name="next_spectra",
    )(limit, own, later, after, *filled)


def exchanged(blocks, axis):
    flat = blocks.reshape(blocks.shape[0], -1, LANES)
    flat = lax.all_to_all(flat, axis, split_axis=0, concat_axis=0, tiled=True)
    return flat.reshape(blocks.shape)


def body(down, back, records, channel_live, offset_limit):
    parts = lax.axis_size("fibre")
    groups = lax.axis_size("freq")
    sums = project(down, records, parts)
    sums = exchanged(sums, "fibre")
    halves = whiten(channel_live[None, :], back, sums, groups)
    halves = exchanged(halves, "freq")
    back_one = [(i, i - 1) for i in range(1, parts)]
    bounds = (0, 32, NB // groups)
    after = [
        lax.ppermute(halves[:, 0, :, low:high], "fibre", back_one)
        for low, high in zip(bounds, bounds[1:])
    ]
    limit = offset_limit[None, :]
    own, later = own_spectra(limit, halves)
    out = None
    for low, piece in zip(bounds, after):
        out = next_spectra(limit, own, later, piece, low, out)
    return out


def solution(mesh):
    down, back = make_tables(mesh.shape["fibre"])
    down = np.concatenate(split_pair(down))
    back = split_pair(back)[0]
    return jax.shard_map(
        functools.partial(body, down, back),
        mesh=mesh,
        in_specs=(P("freq", "fibre", None), P("fibre"), P("fibre")),
        out_specs=P(None, None, "freq", "fibre"),
        check_vma=False,
    )
```

```python
import functools

import jax
import jax.numpy as jnp
import numpy as np
from jax import lax
from jax.experimental import pallas as pl
from jax.experimental.pallas import tpu as pltpu
from jax.sharding import PartitionSpec as P

SAMPLES = 6000
NB = 512
HALF = 32
FIRST_BIN = 60
OFFSETS = 64
BINS = NB + 2 * HALF
RANK = 96
PITCH = 24
LANES = 128
F32 = jnp.float32
BF16 = jnp.bfloat16


def split_pair(values):
    high = values.astype(jnp.bfloat16)
    low = (values - high.astype(np.float64)).astype(jnp.bfloat16)
    return high, low


def make_tables(parts):
    run = SAMPLES // parts
    times = np.arange(run) - (run - 1) / 2
    bins = np.arange(FIRST_BIN - 1, FIRST_BIN + BINS + 1)
    weight = 1.0 + np.arange(len(bins)) / len(bins)
    angles = 2.0 * np.pi * np.outer(times, bins) / SAMPLES
    rows = []
    for wave in (np.cos, np.sin):
        vectors = np.linalg.svd(wave(angles) * weight, full_matrices=False)[0]
        vectors = vectors[:, : RANK // 2]
        rows.append((vectors * np.sign(vectors[run // 2 + 3])).T)
    down = np.concatenate(rows)
    samples = np.arange(SAMPLES)
    kept = np.arange(FIRST_BIN, FIRST_BIN + BINS)
    taper = 0.5 - 0.5 * np.cos(2.0 * np.pi * samples / SAMPLES)
    phase = 2.0 * np.pi * (np.outer(samples, kept) % SAMPLES) / SAMPLES
    table = np.concatenate([np.cos(phase), -np.sin(phase)], axis=1) * taper[:, None]
    back = np.einsum("psj,rs->jpr", table.reshape(parts, run, 2 * BINS), down)
    return down, back.reshape(2 * BINS, parts * RANK)


def project_kernel(down_ref, records_ref, out_ref, held, table, arrived):
    parts, windows = out_ref.shape[:2]
    wide = 4

    def fetch(window):
        return pltpu.make_async_copy(records_ref.at[window], held.at[window], arrived.at[window])

    fetch_table = pltpu.make_async_copy(down_ref, table, arrived.at[windows])
    fetch_table.start()
    for window in range(windows):
        fetch(window).start()
    fetch_table.wait()
    for window in range(windows):
        fetch(window).wait()
        for start in range(0, parts, wide):
            block = held[window, :, start * LANES : (start + wide) * LANES]
            both = jnp.dot(table[...], block, preferred_element_type=F32)
            sums = (both[:RANK] + both[RANK:]).astype(BF16)
            for part in range(wide):
                out_ref[start + part, window] = sums[:, part * LANES : (part + 1) * LANES]


def project(down, records, parts):
    windows, run, channels = records.shape
    down = pltpu.with_memory_space_constraint(down, pltpu.HBM)
    records = pltpu.with_memory_space_constraint(records, pltpu.HBM)
    return pl.pallas_call(
        project_kernel,
        in_specs=[pl.BlockSpec(memory_space=pltpu.HBM)] * 2,
        out_specs=pl.BlockSpec(memory_space=pltpu.VMEM),
        out_shape=jax.ShapeDtypeStruct((parts, windows, RANK, LANES), BF16),
        scratch_shapes=[
            pltpu.VMEM(records.shape, BF16),
            pltpu.VMEM(down.shape, BF16),
            pltpu.SemaphoreType.DMA((windows + 1,)),
        ],
        compiler_params=pltpu.CompilerParams(vmem_limit_bytes=24 * 2**20),
        cost_estimate=pl.CostEstimate(
            flops=4 * RANK * run * channels * windows,
            bytes_accessed=2 * records.size + 2 * parts * windows * RANK * LANES,
            transcendentals=0,
        ),
        name="project",
    )(down, records)


def up_by(values, rows):
    return pltpu.roll(values, values.shape[0] - rows, axis=0)


def whiten_kernel(live_ref, back_ref, sums_ref, out_ref, spectra):
    parts, windows = sums_ref.shape[:2]
    groups = out_ref.shape[0]
    rows = 2 * BINS // 3
    live = live_ref[...].astype(F32)
    live = jnp.concatenate([live, live], axis=1)
    left = lax.broadcasted_iota(jnp.int32, (NB, LANES), 1) < LANES // 2

    def transform(pair):
        columns = jnp.concatenate(
            [sums_ref[:, 2 * pair + i].reshape(parts * RANK, LANES) for i in range(2)], axis=1
        )
        for start in range(0, 2 * BINS, rows):
            spectra[pair % 2, start : start + rows] = jnp.dot(
                back_ref[start : start + rows], columns, preferred_element_type=F32
            )

    transform(0)
    for pair in range(windows // 2):
        if 2 * pair + 2 < windows:
            transform(pair + 1)
        real_part = spectra[pair % 2, :BINS]
        imag_part = spectra[pair % 2, BINS:]
        amplitude = jnp.sqrt(real_part * real_part + imag_part * imag_part)
        total = amplitude
        for reach in (8, 16, 32):
            total = total[: total.shape[0] - reach] + total[reach:]
        for reach in (1, 2, 4):
            total = total + up_by(total, reach)
        smooth = (total[:NB] + amplitude[2 * HALF :]) * (1.0 / (2 * HALF + 1))
        scale = live / (smooth + 1e-06)
        real_part = real_part[HALF : HALF + NB] * scale
        imag_part = imag_part[HALF : HALF + NB] * scale
        for i in range(2):
            real_one = real_part[:, i * LANES : (i + 1) * LANES]
            imag_one = imag_part[:, i * LANES : (i + 1) * LANES]
            first = jnp.where(left, real_one, pltpu.roll(imag_one, LANES // 2, axis=1))
            second = jnp.where(left, pltpu.roll(real_one, LANES // 2, axis=1), imag_one)
            for half, value in enumerate((first, second)):
                value = value.astype(BF16).reshape(groups, NB // groups, LANES)
                out_ref[:, half, 2 * pair + i] = value


def whiten(live, back, sums, groups):
    parts, windows = sums.shape[:2]
    resident = pl.BlockSpec(memory_space=pltpu.VMEM)
    return pl.pallas_call(
        whiten_kernel,
        in_specs=[resident] * 3,
        out_specs=resident,
        out_shape=jax.ShapeDtypeStruct((groups, 2, windows, NB // groups, LANES), BF16),
        scratch_shapes=[pltpu.VMEM((2, 2 * BINS, 2 * LANES), F32)],
        compiler_params=pltpu.CompilerParams(vmem_limit_bytes=28 * 2**20),
        cost_estimate=pl.CostEstimate(
            flops=2 * back.size * windows * LANES,
            bytes_accessed=2 * (back.size + sums.size + 2 * windows * NB * LANES),
            transcendentals=0,
        ),
        name="whiten",
    )(live, back, sums)


def swapped(tiles):
    row = lax.broadcasted_iota(jnp.int32, (8, LANES), 0)
    moved = [tiles[0]] + [pltpu.roll(tiles[j], j, axis=0) for j in range(1, 8)]
    for bit in (1, 2, 4):
        take = (row & bit) != 0
        moved = [jnp.where(take, moved[(j + bit) % 8], moved[j]) for j in range(8)]
    return [moved[0]] + [pltpu.roll(moved[8 - i], 8 - i, axis=0) for i in range(1, 8)]


def own_kernel(limit_ref, halves_ref, part_ref, later_ref, first_all, second_all):
    groups, _, windows, _, _ = halves_ref.shape
    bins = 16
    steps = halves_ref.shape[3] // bins
    every = groups * windows
    half = LANES // 2
    left = lax.broadcasted_iota(jnp.int32, (every, LANES), 1) < half
    offsets = lax.broadcasted_iota(jnp.int32, (OFFSETS, LANES), 0) + 1
    keep = (offsets <= limit_ref[...]).astype(F32)
    lane = lax.broadcasted_iota(jnp.int32, (LANES, LANES), 1)
    turn = (lane[:8] & 7) + 1
    spot = lax.broadcasted_iota(jnp.int32, (8, LANES), 0) + turn

    def skewed(gram):
        gram = jnp.concatenate([gram, jnp.zeros((OFFSETS, LANES), F32)], axis=0)
        for bit in (64, 32, 16, 8):
            rows = min(gram.shape[0] - bit, LANES)
            gram = jnp.where((lane[:rows] & bit) != 0, gram[bit : bit + rows], gram[:rows])
        pieces = [
            jnp.take_along_axis(gram[row : row + 8], spot & 7, axis=0)
            for row in range(0, OFFSETS + 8, 8)
        ]
        merged = [jnp.where(spot < 8, pieces[p], pieces[p + 1]) for p in range(OFFSETS // 8)]
        return jnp.concatenate(merged, axis=0)

    @pl.loop(0, steps)
    def _(step):
        base = pl.multiple_of(step * bins, bins)
        for half_at, kept in ((0, first_all), (1, second_all)):
            values = halves_ref[:, half_at, :, pl.ds(base, bins)].astype(F32)
            values = values.reshape(every, bins, LANES)
            for row in range(every):
                kept[row * PITCH : row * PITCH + bins] = values[row]
        for index in range(bins):
            rows = pl.ds(index, every, stride=PITCH)
            first = first_all[rows, :]
            second = second_all[rows, :]
            turned = pltpu.roll(second, half, axis=1)
            real_x = jnp.where(left, first, turned)
            imag_x = jnp.where(left, pltpu.roll(first, half, axis=1), second)
            partner = jnp.concatenate([real_x, imag_x], axis=0).T.astype(BF16)
            own = jnp.concatenate(
                [
                    jnp.concatenate([real_x, imag_x], axis=1),
                    jnp.concatenate([imag_x, -real_x], axis=1),
                ],
                axis=0,
            ).astype(BF16)
            gram = jnp.dot(partner, own, preferred_element_type=F32)
            for part in range(2):
                value = skewed(gram[:, part * LANES : (part + 1) * LANES]) * keep
                part_ref[base + index, part] = value
            late = jnp.concatenate([second, jnp.where(left, turned, -turned)], axis=0)
            later_ref[base + index] = late.astype(BF16)


def next_kernel(begin, limit_ref, part_ref, later_ref, next_ref, *refs):
    out_ref, next_all, held, sent = refs[-4:]
    groups, windows, _, _ = next_ref.shape
    steps, bins = held.shape[0] // 2, 16
    every = groups * windows
    half = LANES // 2
    lane = lax.broadcasted_iota(jnp.int32, (half, LANES), 1)
    back = half - 1 - (lane & (half - 1))
    row = lax.broadcasted_iota(jnp.int32, (8, LANES), 0)
    spot = row - (back[:8] & 7)

    def lowered(gram):
        for bit in (32, 16, 8):
            moved = jnp.concatenate([jnp.zeros((bit, LANES), F32), gram[: half - bit]], axis=0)
            gram = jnp.where((back & bit) != 0, moved, gram)
        pieces = [jnp.zeros((8, LANES), F32)] + [
            jnp.take_along_axis(gram[at : at + 8], spot & 7, axis=0) for at in range(0, half, 8)
        ]
        merged = [jnp.where(spot >= 0, pieces[p + 1], pieces[p]) for p in range(half // 8)]
        return jnp.concatenate(merged, axis=0)

    offsets = lax.broadcasted_iota(jnp.int32, (OFFSETS, LANES), 0) + 1
    lanes = lax.broadcasted_iota(jnp.int32, (OFFSETS, LANES), 1)
    keep = ((offsets <= limit_ref[...]) & (lanes >= half)).astype(F32)

    def send(step):
        where = pl.ds(pl.multiple_of(begin + step * 8, 8), 8)
        return pltpu.make_async_copy(held.at[step], out_ref.at[:, :, where], sent.at[step])

    @pl.loop(0, steps)
    def _(step):
        base = begin + step * bins
        after_all = next_ref[:, :, pl.ds(pl.multiple_of(step * bins, bins), bins)]
        values = after_all.astype(F32).reshape(every, bins, LANES)
        for row in range(every):
            next_all[row * PITCH : row * PITCH + bins] = values[row]

        def next_part(index):
            after = next_all[pl.ds(index, every, stride=PITCH), :]
            partner = after.astype(BF16).T
            later = later_ref[base + index]
            gram = jnp.dot(partner[:half], later[:every], preferred_element_type=F32)
            gram += jnp.dot(partner[half:], later[every:], preferred_element_type=F32)
            return lowered(gram)

        for start in range(0, bins, 8):
            extra = [next_part(start + at) for at in range(8)]
            for part in range(2):
                for tile in range(0, OFFSETS, 8):
                    sums = []
                    for at in range(8):
                        value = extra[at][tile : tile + 8]
                        if part == 0:
                            value = pltpu.roll(value, half, axis=1)
                        value = value * keep[tile : tile + 8]
                        own = part_ref[base + start + at, part, tile : tile + 8]
                        sums.append(own + value)
                    for at, value in enumerate(swapped(sums)):
                        held[2 * step + start // 8, tile + at, part] = value
            send(2 * step + start // 8).start()

    for step in range(2 * steps):
        send(step).wait()


def own_spectra(limit, halves):
    groups, _, windows, bins, _ = halves.shape
    every = groups * windows
    resident = pl.BlockSpec(memory_space=pltpu.VMEM)
    return pl.pallas_call(
        own_kernel,
        in_specs=[resident] * 2,
        out_specs=[resident] * 2,
        out_shape=[
            jax.ShapeDtypeStruct((bins, 2, OFFSETS, LANES), F32),
            jax.ShapeDtypeStruct((bins, 2 * every, LANES), BF16),
        ],
        scratch_shapes=[pltpu.VMEM(((every + 1) * PITCH, LANES), F32)] * 2,
        compiler_params=pltpu.CompilerParams(vmem_limit_bytes=20 * 2**20),
        cost_estimate=pl.CostEstimate(
            flops=2 * bins * 128 * 96 * 256,
            bytes_accessed=4 * halves.size + 4 * OFFSETS * 2 * bins * LANES,
            transcendentals=0,
        ),
        name="own_spectra",
    )(limit, halves)


def next_spectra(limit, own, later, after, begin, done):
    groups, windows, bins, _ = after.shape
    step = 16
    every = groups * windows
    resident = pl.BlockSpec(memory_space=pltpu.VMEM)
    anywhere = pl.BlockSpec(memory_space=pl.ANY)
    filled = [] if done is None else [done]
    return pl.pallas_call(
        functools.partial(next_kernel, begin),
        in_specs=[resident] * 4 + [anywhere] * len(filled),
        out_specs=anywhere,
        out_shape=jax.ShapeDtypeStruct((OFFSETS, 2, own.shape[0], LANES), F32),
        input_output_aliases={4: 0} if filled else {},
        scratch_shapes=[
            pltpu.VMEM(((every + 1) * PITCH, LANES), F32),
            pltpu.VMEM((bins // 8, OFFSETS, 2, 8, LANES), F32),
            pltpu.SemaphoreType.DMA((bins // 8,)),
        ],
        compiler_params=pltpu.CompilerParams(vmem_limit_bytes=20 * 2**20),
        cost_estimate=pl.CostEstimate(
            flops=2 * bins * 64 * 96 * 128,
            bytes_accessed=2 * after.size + 8 * OFFSETS * 2 * bins * LANES,
            transcendentals=0,
        ),
        name="next_spectra",
    )(limit, own, later, after, *filled)


def exchanged(blocks, axis):
    flat = blocks.reshape(blocks.shape[0], -1, LANES)
    flat = lax.all_to_all(flat, axis, split_axis=0, concat_axis=0, tiled=True)
    return flat.reshape(blocks.shape)


def body(down, back, records, channel_live, offset_limit):
    parts = lax.axis_size("fibre")
    groups = lax.axis_size("freq")
    sums = project(down, records, parts)
    sums = exchanged(sums, "fibre")
    halves = whiten(channel_live[None, :], back, sums, groups)
    halves = exchanged(halves, "freq")
    back_one = [(i, i - 1) for i in range(1, parts)]
    bounds = (0, 32, NB // groups)
    after = [
        lax.ppermute(halves[:, 0, :, low:high], "fibre", back_one)
        for low, high in zip(bounds, bounds[1:])
    ]
    limit = offset_limit[None, :]
    own, later = own_spectra(limit, halves)
    out = None
    for low, piece in zip(bounds, after):
        out = next_spectra(limit, own, later, piece, low, out)
    return out


def solution(mesh):
    down, back = make_tables(mesh.shape["fibre"])
    down = np.concatenate(split_pair(down))
    back = split_pair(back)[0]
    return jax.shard_map(
        functools.partial(body, down, back),
        mesh=mesh,
        in_specs=(P("freq", "fibre", None), P("fibre"), P("fibre")),
        out_specs=P(None, None, "freq", "fibre"),
        check_vma=False,
    )
```

```python
import functools

import jax
import jax.numpy as jnp
import numpy as np
from jax import lax
from jax.experimental import pallas as pl
from jax.experimental.pallas import tpu as pltpu
from jax.sharding import PartitionSpec as P

SAMPLES = 6000
NB = 512
HALF = 32
FIRST_BIN = 60
OFFSETS = 64
BINS = NB + 2 * HALF
RANK = 96
PITCH = 24
LANES = 128
F32 = jnp.float32
BF16 = jnp.bfloat16


def split_pair(values):
    high = values.astype(jnp.bfloat16)
    low = (values - high.astype(np.float64)).astype(jnp.bfloat16)
    return high, low


def make_tables(parts):
    run = SAMPLES // parts
    times = np.arange(run) - (run - 1) / 2
    bins = np.arange(FIRST_BIN - 1, FIRST_BIN + BINS + 1)
    weight = 1.0 + np.arange(len(bins)) / len(bins)
    angles = 2.0 * np.pi * np.outer(times, bins) / SAMPLES
    rows = []
    for wave in (np.cos, np.sin):
        vectors = np.linalg.svd(wave(angles) * weight, full_matrices=False)[0]
        vectors = vectors[:, : RANK // 2]
        rows.append((vectors * np.sign(vectors[run // 2 + 3])).T)
    down = np.concatenate(rows)
    samples = np.arange(SAMPLES)
    kept = np.arange(FIRST_BIN, FIRST_BIN + BINS)
    taper = 0.5 - 0.5 * np.cos(2.0 * np.pi * samples / SAMPLES)
    phase = 2.0 * np.pi * (np.outer(samples, kept) % SAMPLES) / SAMPLES
    table = np.concatenate([np.cos(phase), -np.sin(phase)], axis=1) * taper[:, None]
    back = np.einsum("psj,rs->jpr", table.reshape(parts, run, 2 * BINS), down)
    return down, back.reshape(2 * BINS, parts * RANK)


def project_kernel(down_ref, records_ref, out_ref, held, table, arrived):
    parts, windows = out_ref.shape[:2]
    wide = 4

    def fetch(window):
        return pltpu.make_async_copy(records_ref.at[window], held.at[window], arrived.at[window])

    fetch_table = pltpu.make_async_copy(down_ref, table, arrived.at[windows])
    fetch_table.start()
    for window in range(windows):
        fetch(window).start()
    fetch_table.wait()
    for window in range(windows):
        fetch(window).wait()
        for start in range(0, parts, wide):
            block = held[window, :, start * LANES : (start + wide) * LANES]
            both = jnp.dot(table[...], block, preferred_element_type=F32)
            sums = (both[:RANK] + both[RANK:]).astype(BF16)
            for part in range(wide):
                out_ref[start + part, window] = sums[:, part * LANES : (part + 1) * LANES]


def project(down, records, parts):
    windows, run, channels = records.shape
    down = pltpu.with_memory_space_constraint(down, pltpu.HBM)
    records = pltpu.with_memory_space_constraint(records, pltpu.HBM)
    return pl.pallas_call(
        project_kernel,
        in_specs=[pl.BlockSpec(memory_space=pltpu.HBM)] * 2,
        out_specs=pl.BlockSpec(memory_space=pltpu.VMEM),
        out_shape=jax.ShapeDtypeStruct((parts, windows, RANK, LANES), BF16),
        scratch_shapes=[
            pltpu.VMEM(records.shape, BF16),
            pltpu.VMEM(down.shape, BF16),
            pltpu.SemaphoreType.DMA((windows + 1,)),
        ],
        compiler_params=pltpu.CompilerParams(vmem_limit_bytes=24 * 2**20),
        cost_estimate=pl.CostEstimate(
            flops=4 * RANK * run * channels * windows,
            bytes_accessed=2 * records.size + 2 * parts * windows * RANK * LANES,
            transcendentals=0,
        ),
        name="project",
    )(down, records)


def up_by(values, rows):
    return pltpu.roll(values, values.shape[0] - rows, axis=0)


def whiten_kernel(live_ref, back_ref, sums_ref, out_ref, spectra):
    parts, windows = sums_ref.shape[:2]
    groups = out_ref.shape[0]
    rows = 2 * BINS // 6
    live = live_ref[...].astype(F32)
    live = jnp.concatenate([live, live], axis=1)
    left = lax.broadcasted_iota(jnp.int32, (NB, LANES), 1) < LANES // 2

    def transform(pair):
        columns = jnp.concatenate(
            [sums_ref[:, 2 * pair + i].reshape(parts * RANK, LANES) for i in range(2)], axis=1
        )
        for start in range(0, 2 * BINS, rows):
            spectra[pair % 2, start : start + rows] = jnp.dot(
                back_ref[start : start + rows], columns, preferred_element_type=F32
            )

    transform(0)
    for pair in range(windows // 2):
        if 2 * pair + 2 < windows:
            transform(pair + 1)
        real_part = spectra[pair % 2, :BINS]
        imag_part = spectra[pair % 2, BINS:]
        amplitude = jnp.sqrt(real_part * real_part + imag_part * imag_part)
        total = amplitude
        for reach in (8, 16, 32):
            total = total[: total.shape[0] - reach] + total[reach:]
        for reach in (1, 2, 4):
            total = total + up_by(total, reach)
        smooth = (total[:NB] + amplitude[2 * HALF :]) * (1.0 / (2 * HALF + 1))
        scale = live / (smooth + 1e-06)
        real_part = real_part[HALF : HALF + NB] * scale
        imag_part = imag_part[HALF : HALF + NB] * scale
        for i in range(2):
            real_one = real_part[:, i * LANES : (i + 1) * LANES]
            imag_one = imag_part[:, i * LANES : (i + 1) * LANES]
            first = jnp.where(left, real_one, pltpu.roll(imag_one, LANES // 2, axis=1))
            second = jnp.where(left, pltpu.roll(real_one, LANES // 2, axis=1), imag_one)
            for half, value in enumerate((first, second)):
                value = value.astype(BF16).reshape(groups, NB // groups, LANES)
                out_ref[:, half, 2 * pair + i] = value


def whiten(live, back, sums, groups):
    parts, windows = sums.shape[:2]
    resident = pl.BlockSpec(memory_space=pltpu.VMEM)
    return pl.pallas_call(
        whiten_kernel,
        in_specs=[resident] * 3,
        out_specs=resident,
        out_shape=jax.ShapeDtypeStruct((groups, 2, windows, NB // groups, LANES), BF16),
        scratch_shapes=[pltpu.VMEM((2, 2 * BINS, 2 * LANES), F32)],
        compiler_params=pltpu.CompilerParams(vmem_limit_bytes=28 * 2**20),
        cost_estimate=pl.CostEstimate(
            flops=2 * back.size * windows * LANES,
            bytes_accessed=2 * (back.size + sums.size + 2 * windows * NB * LANES),
            transcendentals=0,
        ),
        name="whiten",
    )(live, back, sums)


def swapped(tiles):
    row = lax.broadcasted_iota(jnp.int32, (8, LANES), 0)
    moved = [tiles[0]] + [pltpu.roll(tiles[j], j, axis=0) for j in range(1, 8)]
    for bit in (1, 2, 4):
        take = (row & bit) != 0
        moved = [jnp.where(take, moved[(j + bit) % 8], moved[j]) for j in range(8)]
    return [moved[0]] + [pltpu.roll(moved[8 - i], 8 - i, axis=0) for i in range(1, 8)]


def own_kernel(limit_ref, halves_ref, part_ref, later_ref, first_all, second_all):
    groups, _, windows, _, _ = halves_ref.shape
    bins = 16
    steps = halves_ref.shape[3] // bins
    every = groups * windows
    half = LANES // 2
    left = lax.broadcasted_iota(jnp.int32, (every, LANES), 1) < half
    offsets = lax.broadcasted_iota(jnp.int32, (OFFSETS, LANES), 0) + 1
    keep = (offsets <= limit_ref[...]).astype(F32)
    lane = lax.broadcasted_iota(jnp.int32, (LANES, LANES), 1)
    turn = (lane[:8] & 7) + 1
    spot = lax.broadcasted_iota(jnp.int32, (8, LANES), 0) + turn

    def skewed(gram):
        gram = jnp.concatenate([gram, jnp.zeros((OFFSETS, LANES), F32)], axis=0)
        for bit in (64, 32, 16, 8):
            rows = min(gram.shape[0] - bit, LANES)
            gram = jnp.where((lane[:rows] & bit) != 0, gram[bit : bit + rows], gram[:rows])
        pieces = [
            jnp.take_along_axis(gram[row : row + 8], spot & 7, axis=0)
            for row in range(0, OFFSETS + 8, 8)
        ]
        merged = [jnp.where(spot < 8, pieces[p], pieces[p + 1]) for p in range(OFFSETS // 8)]
        return jnp.concatenate(merged, axis=0)

    @pl.loop(0, steps)
    def _(step):
        base = pl.multiple_of(step * bins, bins)
        for half_at, kept in ((0, first_all), (1, second_all)):
            values = halves_ref[:, half_at, :, pl.ds(base, bins)].astype(F32)
            values = values.reshape(every, bins, LANES)
            for row in range(every):
                kept[row * PITCH : row * PITCH + bins] = values[row]
        for index in range(bins):
            rows = pl.ds(index, every, stride=PITCH)
            first = first_all[rows, :]
            second = second_all[rows, :]
            turned = pltpu.roll(second, half, axis=1)
            real_x = jnp.where(left, first, turned)
            imag_x = jnp.where(left, pltpu.roll(first, half, axis=1), second)
            partner = jnp.concatenate([real_x, imag_x], axis=0).T.astype(BF16)
            own = jnp.concatenate(
                [
                    jnp.concatenate([real_x, imag_x], axis=1),
                    jnp.concatenate([imag_x, -real_x], axis=1),
                ],
                axis=0,
            ).astype(BF16)
            gram = jnp.dot(partner, own, preferred_element_type=F32)
            for part in range(2):
                value = skewed(gram[:, part * LANES : (part + 1) * LANES]) * keep
                part_ref[base + index, part] = value
            late = jnp.concatenate([second, jnp.where(left, turned, -turned)], axis=0)
            later_ref[base + index] = late.astype(BF16)


def next_kernel(begin, limit_ref, part_ref, later_ref, next_ref, *refs):
    out_ref, next_all, held, sent = refs[-4:]
    groups, windows, _, _ = next_ref.shape
    steps, bins = held.shape[0] // 2, 16
    every = groups * windows
    half = LANES // 2
    lane = lax.broadcasted_iota(jnp.int32, (half, LANES), 1)
    back = half - 1 - (lane & (half - 1))
    row = lax.broadcasted_iota(jnp.int32, (8, LANES), 0)
    spot = row - (back[:8] & 7)

    def lowered(gram):
        for bit in (32, 16, 8):
            moved = jnp.concatenate([jnp.zeros((bit, LANES), F32), gram[: half - bit]], axis=0)
            gram = jnp.where((back & bit) != 0, moved, gram)
        pieces = [jnp.zeros((8, LANES), F32)] + [
            jnp.take_along_axis(gram[at : at + 8], spot & 7, axis=0) for at in range(0, half, 8)
        ]
        merged = [jnp.where(spot >= 0, pieces[p + 1], pieces[p]) for p in range(half // 8)]
        return jnp.concatenate(merged, axis=0)

    offsets = lax.broadcasted_iota(jnp.int32, (OFFSETS, LANES), 0) + 1
    lanes = lax.broadcasted_iota(jnp.int32, (OFFSETS, LANES), 1)
    keep = ((offsets <= limit_ref[...]) & (lanes >= half)).astype(F32)

    def send(step):
        where = pl.ds(pl.multiple_of(begin + step * 8, 8), 8)
        return pltpu.make_async_copy(held.at[step], out_ref.at[:, :, where], sent.at[step])

    @pl.loop(0, steps, unroll=2)
    def _(step):
        base = begin + step * bins
        after_all = next_ref[:, :, pl.ds(pl.multiple_of(step * bins, bins), bins)]
        values = after_all.astype(F32).reshape(every, bins, LANES)
        for row in range(every):
            next_all[row * PITCH : row * PITCH + bins] = values[row]

        def next_part(index):
            after = next_all[pl.ds(index, every, stride=PITCH), :]
            partner = after.astype(BF16).T
            later = later_ref[base + index]
            gram = jnp.dot(partner[:half], later[:every], preferred_element_type=F32)
            gram += jnp.dot(partner[half:], later[every:], preferred_element_type=F32)
            return lowered(gram)

        for start in range(0, bins, 8):
            extra = [next_part(start + at) for at in range(8)]
            for part in range(2):
                for tile in range(0, OFFSETS, 8):
                    sums = []
                    for at in range(8):
                        value = extra[at][tile : tile + 8]
                        if part == 0:
                            value = pltpu.roll(value, half, axis=1)
                        value = value * keep[tile : tile + 8]
                        own = part_ref[base + start + at, part, tile : tile + 8]
                        sums.append(own + value)
                    for at, value in enumerate(swapped(sums)):
                        held[2 * step + start // 8, tile + at, part] = value
            send(2 * step + start // 8).start()

    for step in range(2 * steps):
        send(step).wait()


def own_spectra(limit, halves):
    groups, _, windows, bins, _ = halves.shape
    every = groups * windows
    resident = pl.BlockSpec(memory_space=pltpu.VMEM)
    return pl.pallas_call(
        own_kernel,
        in_specs=[resident] * 2,
        out_specs=[resident] * 2,
        out_shape=[
            jax.ShapeDtypeStruct((bins, 2, OFFSETS, LANES), F32),
            jax.ShapeDtypeStruct((bins, 2 * every, LANES), BF16),
        ],
        scratch_shapes=[pltpu.VMEM(((every + 1) * PITCH, LANES), F32)] * 2,
        compiler_params=pltpu.CompilerParams(vmem_limit_bytes=20 * 2**20),
        cost_estimate=pl.CostEstimate(
            flops=2 * bins * 128 * 96 * 256,
            bytes_accessed=4 * halves.size + 4 * OFFSETS * 2 * bins * LANES,
            transcendentals=0,
        ),
        name="own_spectra",
    )(limit, halves)


def next_spectra(limit, own, later, after, begin, done):
    groups, windows, bins, _ = after.shape
    step = 16
    every = groups * windows
    resident = pl.BlockSpec(memory_space=pltpu.VMEM)
    anywhere = pl.BlockSpec(memory_space=pl.ANY)
    filled = [] if done is None else [done]
    return pl.pallas_call(
        functools.partial(next_kernel, begin),
        in_specs=[resident] * 4 + [anywhere] * len(filled),
        out_specs=anywhere,
        out_shape=jax.ShapeDtypeStruct((OFFSETS, 2, own.shape[0], LANES), F32),
        input_output_aliases={4: 0} if filled else {},
        scratch_shapes=[
            pltpu.VMEM(((every + 1) * PITCH, LANES), F32),
            pltpu.VMEM((bins // 8, OFFSETS, 2, 8, LANES), F32),
            pltpu.SemaphoreType.DMA((bins // 8,)),
        ],
        compiler_params=pltpu.CompilerParams(vmem_limit_bytes=20 * 2**20),
        cost_estimate=pl.CostEstimate(
            flops=2 * bins * 64 * 96 * 128,
            bytes_accessed=2 * after.size + 8 * OFFSETS * 2 * bins * LANES,
            transcendentals=0,
        ),
        name="next_spectra",
    )(limit, own, later, after, *filled)


def exchanged(blocks, axis):
    flat = blocks.reshape(blocks.shape[0], -1, LANES)
    flat = lax.all_to_all(flat, axis, split_axis=0, concat_axis=0, tiled=True)
    return flat.reshape(blocks.shape)


def body(down, back, records, channel_live, offset_limit):
    parts = lax.axis_size("fibre")
    groups = lax.axis_size("freq")
    sums = project(down, records, parts)
    sums = exchanged(sums, "fibre")
    halves = whiten(channel_live[None, :], back, sums, groups)
    halves = exchanged(halves, "freq")
    back_one = [(i, i - 1) for i in range(1, parts)]
    bounds = (0, 32, NB // groups)
    after = [
        lax.ppermute(halves[:, 0, :, low:high], "fibre", back_one)
        for low, high in zip(bounds, bounds[1:])
    ]
    limit = offset_limit[None, :]
    own, later = own_spectra(limit, halves)
    out = None
    for low, piece in zip(bounds, after):
        out = next_spectra(limit, own, later, piece, low, out)
    return out


def solution(mesh):
    down, back = make_tables(mesh.shape["fibre"])
    down = np.concatenate(split_pair(down))
    back = split_pair(back)[0]
    return jax.shard_map(
        functools.partial(body, down, back),
        mesh=mesh,
        in_specs=(P("freq", "fibre", None), P("fibre"), P("fibre")),
        out_specs=P(None, None, "freq", "fibre"),
        check_vma=False,
    )
```

```python
import functools

import jax
import jax.numpy as jnp
import numpy as np
from jax import lax
from jax.experimental import pallas as pl
from jax.experimental.pallas import tpu as pltpu
from jax.sharding import PartitionSpec as P

SAMPLES = 6000
NB = 512
HALF = 32
FIRST_BIN = 60
OFFSETS = 64
BINS = NB + 2 * HALF
RANK = 96
PITCH = 24
LANES = 128
F32 = jnp.float32
BF16 = jnp.bfloat16


def split_pair(values):
    high = values.astype(jnp.bfloat16)
    low = (values - high.astype(np.float64)).astype(jnp.bfloat16)
    return high, low


def make_tables(parts):
    run = SAMPLES // parts
    times = np.arange(run) - (run - 1) / 2
    bins = np.arange(FIRST_BIN - 1, FIRST_BIN + BINS + 1)
    weight = 1.0 + np.arange(len(bins)) / len(bins)
    angles = 2.0 * np.pi * np.outer(times, bins) / SAMPLES
    rows = []
    for wave in (np.cos, np.sin):
        vectors = np.linalg.svd(wave(angles) * weight, full_matrices=False)[0]
        vectors = vectors[:, : RANK // 2]
        rows.append((vectors * np.sign(vectors[run // 2 + 3])).T)
    down = np.concatenate(rows)
    samples = np.arange(SAMPLES)
    kept = np.arange(FIRST_BIN, FIRST_BIN + BINS)
    taper = 0.5 - 0.5 * np.cos(2.0 * np.pi * samples / SAMPLES)
    phase = 2.0 * np.pi * (np.outer(samples, kept) % SAMPLES) / SAMPLES
    table = np.concatenate([np.cos(phase), -np.sin(phase)], axis=1) * taper[:, None]
    back = np.einsum("psj,rs->jpr", table.reshape(parts, run, 2 * BINS), down)
    return down, back.reshape(2 * BINS, parts * RANK)


def project_kernel(down_ref, records_ref, out_ref, held, table, arrived):
    parts, windows = out_ref.shape[:2]
    wide = 4

    def fetch(window):
        return pltpu.make_async_copy(records_ref.at[window], held.at[window], arrived.at[window])

    fetch_table = pltpu.make_async_copy(down_ref, table, arrived.at[windows])
    fetch_table.start()
    for window in range(windows):
        fetch(window).start()
    fetch_table.wait()
    for window in range(windows):
        fetch(window).wait()
        for start in range(0, parts, wide):
            block = held[window, :, start * LANES : (start + wide) * LANES]
            both = jnp.dot(table[...], block, preferred_element_type=F32)
            sums = (both[:RANK] + both[RANK:]).astype(BF16)
            for part in range(wide):
                out_ref[start + part, window] = sums[:, part * LANES : (part + 1) * LANES]


def project(down, records, parts):
    windows, run, channels = records.shape
    down = pltpu.with_memory_space_constraint(down, pltpu.HBM)
    records = pltpu.with_memory_space_constraint(records, pltpu.HBM)
    return pl.pallas_call(
        project_kernel,
        in_specs=[pl.BlockSpec(memory_space=pltpu.HBM)] * 2,
        out_specs=pl.BlockSpec(memory_space=pltpu.VMEM),
        out_shape=jax.ShapeDtypeStruct((parts, windows, RANK, LANES), BF16),
        scratch_shapes=[
            pltpu.VMEM(records.shape, BF16),
            pltpu.VMEM(down.shape, BF16),
            pltpu.SemaphoreType.DMA((windows + 1,)),
        ],
        compiler_params=pltpu.CompilerParams(vmem_limit_bytes=24 * 2**20),
        cost_estimate=pl.CostEstimate(
            flops=4 * RANK * run * channels * windows,
            bytes_accessed=2 * records.size + 2 * parts * windows * RANK * LANES,
            transcendentals=0,
        ),
        name="project",
    )(down, records)


def up_by(values, rows):
    return pltpu.roll(values, values.shape[0] - rows, axis=0)


def whiten_kernel(live_ref, back_ref, sums_ref, out_ref, spectra):
    parts, windows = sums_ref.shape[:2]
    groups = out_ref.shape[0]
    rows = 2 * BINS // 6
    live = live_ref[...].astype(F32)
    live = jnp.concatenate([live, live], axis=1)
    left = lax.broadcasted_iota(jnp.int32, (NB, LANES), 1) < LANES // 2

    def transform(pair):
        columns = jnp.concatenate(
            [sums_ref[:, 2 * pair + i].reshape(parts * RANK, LANES) for i in range(2)], axis=1
        )
        for start in range(0, 2 * BINS, rows):
            spectra[pair % 2, start : start + rows] = jnp.dot(
                back_ref[start : start + rows], columns, preferred_element_type=F32
            )

    transform(0)
    for pair in range(windows // 2):
        if 2 * pair + 2 < windows:
            transform(pair + 1)
        real_part = spectra[pair % 2, :BINS]
        imag_part = spectra[pair % 2, BINS:]
        amplitude = jnp.sqrt(real_part * real_part + imag_part * imag_part)
        total = amplitude
        for reach in (8, 16, 32):
            total = total[: total.shape[0] - reach] + total[reach:]
        for reach in (1, 2, 4):
            total = total + up_by(total, reach)
        smooth = (total[:NB] + amplitude[2 * HALF :]) * (1.0 / (2 * HALF + 1))
        scale = live / (smooth + 1e-06)
        real_part = real_part[HALF : HALF + NB] * scale
        imag_part = imag_part[HALF : HALF + NB] * scale
        for i in range(2):
            real_one = real_part[:, i * LANES : (i + 1) * LANES]
            imag_one = imag_part[:, i * LANES : (i + 1) * LANES]
            first = jnp.where(left, real_one, pltpu.roll(imag_one, LANES // 2, axis=1))
            second = jnp.where(left, pltpu.roll(real_one, LANES // 2, axis=1), imag_one)
            for half, value in enumerate((first, second)):
                value = value.astype(BF16).reshape(groups, NB // groups, LANES)
                out_ref[:, half, 2 * pair + i] = value


def whiten(live, back, sums, groups):
    parts, windows = sums.shape[:2]
    resident = pl.BlockSpec(memory_space=pltpu.VMEM)
    return pl.pallas_call(
        whiten_kernel,
        in_specs=[resident] * 3,
        out_specs=resident,
        out_shape=jax.ShapeDtypeStruct((groups, 2, windows, NB // groups, LANES), BF16),
        scratch_shapes=[pltpu.VMEM((2, 2 * BINS, 2 * LANES), F32)],
        compiler_params=pltpu.CompilerParams(vmem_limit_bytes=28 * 2**20),
        cost_estimate=pl.CostEstimate(
            flops=2 * back.size * windows * LANES,
            bytes_accessed=2 * (back.size + sums.size + 2 * windows * NB * LANES),
            transcendentals=0,
        ),
        name="whiten",
    )(live, back, sums)


def swapped(tiles):
    row = lax.broadcasted_iota(jnp.int32, (8, LANES), 0)
    moved = [tiles[0]] + [pltpu.roll(tiles[j], j, axis=0) for j in range(1, 8)]
    for bit in (1, 2, 4):
        take = (row & bit) != 0
        moved = [jnp.where(take, moved[(j + bit) % 8], moved[j]) for j in range(8)]
    return [moved[0]] + [pltpu.roll(moved[8 - i], 8 - i, axis=0) for i in range(1, 8)]


def own_kernel(limit_ref, halves_ref, part_ref, later_ref, first_all, second_all):
    groups, _, windows, _, _ = halves_ref.shape
    bins = 16
    steps = halves_ref.shape[3] // bins
    every = groups * windows
    half = LANES // 2
    left = lax.broadcasted_iota(jnp.int32, (every, LANES), 1) < half
    offsets = lax.broadcasted_iota(jnp.int32, (OFFSETS, LANES), 0) + 1
    keep = (offsets <= limit_ref[...]).astype(F32)
    lane = lax.broadcasted_iota(jnp.int32, (LANES, LANES), 1)
    turn = (lane[:8] & 7) + 1
    spot = lax.broadcasted_iota(jnp.int32, (8, LANES), 0) + turn

    def skewed(gram):
        gram = jnp.concatenate([gram, jnp.zeros((OFFSETS, LANES), F32)], axis=0)
        for bit in (64, 32, 16, 8):
            rows = min(gram.shape[0] - bit, LANES)
            gram = jnp.where((lane[:rows] & bit) != 0, gram[bit : bit + rows], gram[:rows])
        pieces = [
            jnp.take_along_axis(gram[row : row + 8], spot & 7, axis=0)
            for row in range(0, OFFSETS + 8, 8)
        ]
        merged = [jnp.where(spot < 8, pieces[p], pieces[p + 1]) for p in range(OFFSETS // 8)]
        return jnp.concatenate(merged, axis=0)

    @pl.loop(0, steps)
    def _(step):
        base = pl.multiple_of(step * bins, bins)
        for half_at, kept in ((0, first_all), (1, second_all)):
            values = halves_ref[:, half_at, :, pl.ds(base, bins)].astype(F32)
            values = values.reshape(every, bins, LANES)
            for row in range(every):
                kept[row * PITCH : row * PITCH + bins] = values[row]
        for index in range(bins):
            rows = pl.ds(index, every, stride=PITCH)
            first = first_all[rows, :]
            second = second_all[rows, :]
            turned = pltpu.roll(second, half, axis=1)
            real_x = jnp.where(left, first, turned)
            imag_x = jnp.where(left, pltpu.roll(first, half, axis=1), second)
            partner = jnp.concatenate([real_x, imag_x], axis=0).T.astype(BF16)
            own = jnp.concatenate(
                [
                    jnp.concatenate([real_x, imag_x], axis=1),
                    jnp.concatenate([imag_x, -real_x], axis=1),
                ],
                axis=0,
            ).astype(BF16)
            gram = jnp.dot(partner, own, preferred_element_type=F32)
            for part in range(2):
                value = skewed(gram[:, part * LANES : (part + 1) * LANES]) * keep
                part_ref[base + index, part] = value
            late = jnp.concatenate([second, jnp.where(left, turned, -turned)], axis=0)
            later_ref[base + index] = late.astype(BF16)


def next_kernel(begin, limit_ref, part_ref, later_ref, next_ref, *refs):
    out_ref, next_all, held, sent = refs[-4:]
    groups, windows, _, _ = next_ref.shape
    steps, bins = held.shape[0] // 2, 16
    every = groups * windows
    half = LANES // 2
    lane = lax.broadcasted_iota(jnp.int32, (half, LANES), 1)
    back = half - 1 - (lane & (half - 1))
    row = lax.broadcasted_iota(jnp.int32, (8, LANES), 0)
    spot = row - (back[:8] & 7)

    def lowered(gram):
        for bit in (32, 16, 8):
            moved = jnp.concatenate([jnp.zeros((bit, LANES), F32), gram[: half - bit]], axis=0)
            gram = jnp.where((back & bit) != 0, moved, gram)
        pieces = [jnp.zeros((8, LANES), F32)] + [
            jnp.take_along_axis(gram[at : at + 8], spot & 7, axis=0) for at in range(0, half, 8)
        ]
        merged = [jnp.where(spot >= 0, pieces[p + 1], pieces[p]) for p in range(half // 8)]
        return jnp.concatenate(merged, axis=0)

    offsets = lax.broadcasted_iota(jnp.int32, (OFFSETS, LANES), 0) + 1
    lanes = lax.broadcasted_iota(jnp.int32, (OFFSETS, LANES), 1)
    keep = ((offsets <= limit_ref[...]) & (lanes >= half)).astype(F32)

    def send(step):
        where = pl.ds(pl.multiple_of(begin + step * 8, 8), 8)
        return pltpu.make_async_copy(held.at[step], out_ref.at[:, :, where], sent.at[step])

    @pl.loop(0, steps, unroll=steps)
    def _(step):
        base = begin + step * bins
        after_all = next_ref[:, :, pl.ds(pl.multiple_of(step * bins, bins), bins)]
        values = after_all.astype(F32).reshape(every, bins, LANES)
        for row in range(every):
            next_all[row * PITCH : row * PITCH + bins] = values[row]

        def next_part(index):
            after = next_all[pl.ds(index, every, stride=PITCH), :]
            partner = after.astype(BF16).T
            later = later_ref[base + index]
            gram = jnp.dot(partner[:half], later[:every], preferred_element_type=F32)
            gram += jnp.dot(partner[half:], later[every:], preferred_element_type=F32)
            return lowered(gram)

        for start in range(0, bins, 8):
            extra = [next_part(start + at) for at in range(8)]
            for part in range(2):
                for tile in range(0, OFFSETS, 8):
                    sums = []
                    for at in range(8):
                        value = extra[at][tile : tile + 8]
                        if part == 0:
                            value = pltpu.roll(value, half, axis=1)
                        value = value * keep[tile : tile + 8]
                        own = part_ref[base + start + at, part, tile : tile + 8]
                        sums.append(own + value)
                    for at, value in enumerate(swapped(sums)):
                        held[2 * step + start // 8, tile + at, part] = value
            send(2 * step + start // 8).start()

    for step in range(2 * steps):
        send(step).wait()


def own_spectra(limit, halves):
    groups, _, windows, bins, _ = halves.shape
    every = groups * windows
    resident = pl.BlockSpec(memory_space=pltpu.VMEM)
    return pl.pallas_call(
        own_kernel,
        in_specs=[resident] * 2,
        out_specs=[resident] * 2,
        out_shape=[
            jax.ShapeDtypeStruct((bins, 2, OFFSETS, LANES), F32),
            jax.ShapeDtypeStruct((bins, 2 * every, LANES), BF16),
        ],
        scratch_shapes=[pltpu.VMEM(((every + 1) * PITCH, LANES), F32)] * 2,
        compiler_params=pltpu.CompilerParams(vmem_limit_bytes=20 * 2**20),
        cost_estimate=pl.CostEstimate(
            flops=2 * bins * 128 * 96 * 256,
            bytes_accessed=4 * halves.size + 4 * OFFSETS * 2 * bins * LANES,
            transcendentals=0,
        ),
        name="own_spectra",
    )(limit, halves)


def next_spectra(limit, own, later, after, begin, done):
    groups, windows, bins, _ = after.shape
    step = 16
    every = groups * windows
    resident = pl.BlockSpec(memory_space=pltpu.VMEM)
    anywhere = pl.BlockSpec(memory_space=pl.ANY)
    filled = [] if done is None else [done]
    return pl.pallas_call(
        functools.partial(next_kernel, begin),
        in_specs=[resident] * 4 + [anywhere] * len(filled),
        out_specs=anywhere,
        out_shape=jax.ShapeDtypeStruct((OFFSETS, 2, own.shape[0], LANES), F32),
        input_output_aliases={4: 0} if filled else {},
        scratch_shapes=[
            pltpu.VMEM(((every + 1) * PITCH, LANES), F32),
            pltpu.VMEM((bins // 8, OFFSETS, 2, 8, LANES), F32),
            pltpu.SemaphoreType.DMA((bins // 8,)),
        ],
        compiler_params=pltpu.CompilerParams(vmem_limit_bytes=20 * 2**20),
        cost_estimate=pl.CostEstimate(
            flops=2 * bins * 64 * 96 * 128,
            bytes_accessed=2 * after.size + 8 * OFFSETS * 2 * bins * LANES,
            transcendentals=0,
        ),
        name="next_spectra",
    )(limit, own, later, after, *filled)


def exchanged(blocks, axis):
    flat = blocks.reshape(blocks.shape[0], -1, LANES)
    flat = lax.all_to_all(flat, axis, split_axis=0, concat_axis=0, tiled=True)
    return flat.reshape(blocks.shape)


def body(down, back, records, channel_live, offset_limit):
    parts = lax.axis_size("fibre")
    groups = lax.axis_size("freq")
    sums = project(down, records, parts)
    sums = exchanged(sums, "fibre")
    halves = whiten(channel_live[None, :], back, sums, groups)
    halves = exchanged(halves, "freq")
    back_one = [(i, i - 1) for i in range(1, parts)]
    bounds = (0, 48, NB // groups)
    after = [
        lax.ppermute(halves[:, 0, :, low:high], "fibre", back_one)
        for low, high in zip(bounds, bounds[1:])
    ]
    limit = offset_limit[None, :]
    own, later = own_spectra(limit, halves)
    out = None
    for low, piece in zip(bounds, after):
        out = next_spectra(limit, own, later, piece, low, out)
    return out


def solution(mesh):
    down, back = make_tables(mesh.shape["fibre"])
    down = np.concatenate(split_pair(down))
    back = split_pair(back)[0]
    return jax.shard_map(
        functools.partial(body, down, back),
        mesh=mesh,
        in_specs=(P("freq", "fibre", None), P("fibre"), P("fibre")),
        out_specs=P(None, None, "freq", "fibre"),
        check_vma=False,
    )
```

```python
import functools

import jax
import jax.numpy as jnp
import numpy as np
from jax import lax
from jax.experimental import pallas as pl
from jax.experimental.pallas import tpu as pltpu
from jax.sharding import PartitionSpec as P

SAMPLES = 6000
NB = 512
HALF = 32
FIRST_BIN = 60
OFFSETS = 64
BINS = NB + 2 * HALF
RANK = 96
PITCH = 24
LANES = 128
F32 = jnp.float32
BF16 = jnp.bfloat16


def split_pair(values):
    high = values.astype(jnp.bfloat16)
    low = (values - high.astype(np.float64)).astype(jnp.bfloat16)
    return high, low


def make_tables(parts):
    run = SAMPLES // parts
    times = np.arange(run) - (run - 1) / 2
    bins = np.arange(FIRST_BIN - 1, FIRST_BIN + BINS + 1)
    weight = 1.0 + np.arange(len(bins)) / len(bins)
    angles = 2.0 * np.pi * np.outer(times, bins) / SAMPLES
    rows = []
    for wave in (np.cos, np.sin):
        vectors = np.linalg.svd(wave(angles) * weight, full_matrices=False)[0]
        vectors = vectors[:, : RANK // 2]
        rows.append((vectors * np.sign(vectors[run // 2 + 3])).T)
    down = np.concatenate(rows)
    samples = np.arange(SAMPLES)
    kept = np.arange(FIRST_BIN, FIRST_BIN + BINS)
    taper = 0.5 - 0.5 * np.cos(2.0 * np.pi * samples / SAMPLES)
    phase = 2.0 * np.pi * (np.outer(samples, kept) % SAMPLES) / SAMPLES
    table = np.concatenate([np.cos(phase), -np.sin(phase)], axis=1) * taper[:, None]
    back = np.einsum("psj,rs->jpr", table.reshape(parts, run, 2 * BINS), down)
    return down, back.reshape(2 * BINS, parts * RANK)


def project_kernel(down_ref, records_ref, out_ref, held, table, arrived):
    parts, windows = out_ref.shape[:2]
    wide = 4

    def fetch(window):
        return pltpu.make_async_copy(records_ref.at[window], held.at[window], arrived.at[window])

    fetch_table = pltpu.make_async_copy(down_ref, table, arrived.at[windows])
    fetch_table.start()
    for window in range(windows):
        fetch(window).start()
    fetch_table.wait()
    for window in range(windows):
        fetch(window).wait()
        for start in range(0, parts, wide):
            block = held[window, :, start * LANES : (start + wide) * LANES]
            both = jnp.dot(table[...], block, preferred_element_type=F32)
            sums = (both[:RANK] + both[RANK:]).astype(BF16)
            for part in range(wide):
                out_ref[start + part, window] = sums[:, part * LANES : (part + 1) * LANES]


def project(down, records, parts):
    windows, run, channels = records.shape
    down = pltpu.with_memory_space_constraint(down, pltpu.HBM)
    records = pltpu.with_memory_space_constraint(records, pltpu.HBM)
    return pl.pallas_call(
        project_kernel,
        in_specs=[pl.BlockSpec(memory_space=pltpu.HBM)] * 2,
        out_specs=pl.BlockSpec(memory_space=pltpu.VMEM),
        out_shape=jax.ShapeDtypeStruct((parts, windows, RANK, LANES), BF16),
        scratch_shapes=[
            pltpu.VMEM(records.shape, BF16),
            pltpu.VMEM(down.shape, BF16),
            pltpu.SemaphoreType.DMA((windows + 1,)),
        ],
        compiler_params=pltpu.CompilerParams(vmem_limit_bytes=24 * 2**20),
        cost_estimate=pl.CostEstimate(
            flops=4 * RANK * run * channels * windows,
            bytes_accessed=2 * records.size + 2 * parts * windows * RANK * LANES,
            transcendentals=0,
        ),
        name="project",
    )(down, records)


def up_by(values, rows):
    return pltpu.roll(values, values.shape[0] - rows, axis=0)


def whiten_kernel(live_ref, back_ref, sums_ref, out_ref, spectra):
    parts, windows = sums_ref.shape[:2]
    groups = out_ref.shape[0]
    rows = 2 * BINS // 6
    live = live_ref[...].astype(F32)
    live = jnp.concatenate([live, live], axis=1)
    left = lax.broadcasted_iota(jnp.int32, (NB, LANES), 1) < LANES // 2

    def transform(pair):
        columns = jnp.concatenate(
            [sums_ref[:, 2 * pair + i].reshape(parts * RANK, LANES) for i in range(2)], axis=1
        )
        for start in range(0, 2 * BINS, rows):
            spectra[pair % 2, start : start + rows] = jnp.dot(
                back_ref[start : start + rows], columns, preferred_element_type=F32
            )

    transform(0)
    for pair in range(windows // 2):
        if 2 * pair + 2 < windows:
            transform(pair + 1)
        real_part = spectra[pair % 2, :BINS]
        imag_part = spectra[pair % 2, BINS:]
        amplitude = jnp.sqrt(real_part * real_part + imag_part * imag_part)
        total = amplitude
        for reach in (8, 16, 32):
            total = total[: total.shape[0] - reach] + total[reach:]
        for reach in (1, 2, 4):
            total = total + up_by(total, reach)
        smooth = (total[:NB] + amplitude[2 * HALF :]) * (1.0 / (2 * HALF + 1))
        scale = live / (smooth + 1e-06)
        real_part = real_part[HALF : HALF + NB] * scale
        imag_part = imag_part[HALF : HALF + NB] * scale
        for i in range(2):
            real_one = real_part[:, i * LANES : (i + 1) * LANES]
            imag_one = imag_part[:, i * LANES : (i + 1) * LANES]
            first = jnp.where(left, real_one, pltpu.roll(imag_one, LANES // 2, axis=1))
            second = jnp.where(left, pltpu.roll(real_one, LANES // 2, axis=1), imag_one)
            for half, value in enumerate((first, second)):
                value = value.astype(BF16).reshape(groups, NB // groups, LANES)
                out_ref[:, half, 2 * pair + i] = value


def whiten(live, back, sums, groups):
    parts, windows = sums.shape[:2]
    resident = pl.BlockSpec(memory_space=pltpu.VMEM)
    return pl.pallas_call(
        whiten_kernel,
        in_specs=[resident] * 3,
        out_specs=resident,
        out_shape=jax.ShapeDtypeStruct((groups, 2, windows, NB // groups, LANES), BF16),
        scratch_shapes=[pltpu.VMEM((2, 2 * BINS, 2 * LANES), F32)],
        compiler_params=pltpu.CompilerParams(vmem_limit_bytes=28 * 2**20),
        cost_estimate=pl.CostEstimate(
            flops=2 * back.size * windows * LANES,
            bytes_accessed=2 * (back.size + sums.size + 2 * windows * NB * LANES),
            transcendentals=0,
        ),
        name="whiten",
    )(live, back, sums)


def swapped(tiles):
    row = lax.broadcasted_iota(jnp.int32, (8, LANES), 0)
    moved = [tiles[0]] + [pltpu.roll(tiles[j], j, axis=0) for j in range(1, 8)]
    for bit in (1, 2, 4):
        take = (row & bit) != 0
        moved = [jnp.where(take, moved[(j + bit) % 8], moved[j]) for j in range(8)]
    return [moved[0]] + [pltpu.roll(moved[8 - i], 8 - i, axis=0) for i in range(1, 8)]


def own_kernel(limit_ref, halves_ref, part_ref, later_ref, first_all, second_all):
    groups, _, windows, _, _ = halves_ref.shape
    bins = 16
    steps = halves_ref.shape[3] // bins
    every = groups * windows
    half = LANES // 2
    left = lax.broadcasted_iota(jnp.int32, (every, LANES), 1) < half
    offsets = lax.broadcasted_iota(jnp.int32, (OFFSETS, LANES), 0) + 1
    keep = (offsets <= limit_ref[...]).astype(F32)
    lane = lax.broadcasted_iota(jnp.int32, (LANES, LANES), 1)
    turn = (lane[:8] & 7) + 1
    spot = lax.broadcasted_iota(jnp.int32, (8, LANES), 0) + turn

    def skewed(gram):
        gram = jnp.concatenate([gram, jnp.zeros((OFFSETS, LANES), F32)], axis=0)
        for bit in (64, 32, 16, 8):
            rows = min(gram.shape[0] - bit, LANES)
            gram = jnp.where((lane[:rows] & bit) != 0, gram[bit : bit + rows], gram[:rows])
        pieces = [
            jnp.take_along_axis(gram[row : row + 8], spot & 7, axis=0)
            for row in range(0, OFFSETS + 8, 8)
        ]
        merged = [jnp.where(spot < 8, pieces[p], pieces[p + 1]) for p in range(OFFSETS // 8)]
        return jnp.concatenate(merged, axis=0)

    @pl.loop(0, steps)
    def _(step):
        base = pl.multiple_of(step * bins, bins)
        for half_at, kept in ((0, first_all), (1, second_all)):
            values = halves_ref[:, half_at, :, pl.ds(base, bins)].astype(F32)
            values = values.reshape(every, bins, LANES)
            for row in range(every):
                kept[row * PITCH : row * PITCH + bins] = values[row]
        for index in range(bins):
            rows = pl.ds(index, every, stride=PITCH)
            first = first_all[rows, :]
            second = second_all[rows, :]
            turned = pltpu.roll(second, half, axis=1)
            real_x = jnp.where(left, first, turned)
            imag_x = jnp.where(left, pltpu.roll(first, half, axis=1), second)
            partner = jnp.concatenate([real_x, imag_x], axis=0).T.astype(BF16)
            own = jnp.concatenate(
                [
                    jnp.concatenate([real_x, imag_x], axis=1),
                    jnp.concatenate([imag_x, -real_x], axis=1),
                ],
                axis=0,
            ).astype(BF16)
            gram = jnp.dot(partner, own, preferred_element_type=F32)
            for part in range(2):
                value = skewed(gram[:, part * LANES : (part + 1) * LANES]) * keep
                part_ref[base + index, part] = value
            late = jnp.concatenate([second, jnp.where(left, turned, -turned)], axis=0)
            later_ref[base + index] = late.astype(BF16)


def next_kernel(begin, limit_ref, part_ref, later_ref, next_ref, *refs):
    out_ref, next_all, held, sent = refs[-4:]
    groups, windows, _, _ = next_ref.shape
    steps, bins = held.shape[0] // 2, 16
    every = groups * windows
    half = LANES // 2
    lane = lax.broadcasted_iota(jnp.int32, (half, LANES), 1)
    back = half - 1 - (lane & (half - 1))
    row = lax.broadcasted_iota(jnp.int32, (8, LANES), 0)
    spot = row - (back[:8] & 7)

    def lowered(gram):
        for bit in (32, 16, 8):
            moved = jnp.concatenate([jnp.zeros((bit, LANES), F32), gram[: half - bit]], axis=0)
            gram = jnp.where((back & bit) != 0, moved, gram)
        pieces = [jnp.zeros((8, LANES), F32)] + [
            jnp.take_along_axis(gram[at : at + 8], spot & 7, axis=0) for at in range(0, half, 8)
        ]
        merged = [jnp.where(spot >= 0, pieces[p + 1], pieces[p]) for p in range(half // 8)]
        return jnp.concatenate(merged, axis=0)

    offsets = lax.broadcasted_iota(jnp.int32, (OFFSETS, LANES), 0) + 1
    lanes = lax.broadcasted_iota(jnp.int32, (OFFSETS, LANES), 1)
    keep = ((offsets <= limit_ref[...]) & (lanes >= half)).astype(F32)

    def send(step, part):
        where = pl.ds(pl.multiple_of(begin + step * 8, 8), 8)
        return pltpu.make_async_copy(
            held.at[step, part], out_ref.at[:, part, where], sent.at[step, part]
        )

    @pl.loop(0, steps, unroll=2)
    def _(step):
        base = begin + step * bins
        after_all = next_ref[:, :, pl.ds(pl.multiple_of(step * bins, bins), bins)]
        values = after_all.astype(F32).reshape(every, bins, LANES)
        for row in range(every):
            next_all[row * PITCH : row * PITCH + bins] = values[row]

        def next_part(index):
            after = next_all[pl.ds(index, every, stride=PITCH), :]
            partner = after.astype(BF16).T
            later = later_ref[base + index]
            gram = jnp.dot(partner[:half], later[:every], preferred_element_type=F32)
            gram += jnp.dot(partner[half:], later[every:], preferred_element_type=F32)
            return lowered(gram)

        for start in range(0, bins, 8):
            extra = [next_part(start + at) for at in range(8)]
            for part in range(2):
                for tile in range(0, OFFSETS, 8):
                    sums = []
                    for at in range(8):
                        value = extra[at][tile : tile + 8]
                        if part == 0:
                            value = pltpu.roll(value, half, axis=1)
                        value = value * keep[tile : tile + 8]
                        own = part_ref[base + start + at, part, tile : tile + 8]
                        sums.append(own + value)
                    for at, value in enumerate(swapped(sums)):
                        held[2 * step + start // 8, part, tile + at] = value
                send(2 * step + start // 8, part).start()

    for step in range(2 * steps):
        for part in range(2):
            send(step, part).wait()


def own_spectra(limit, halves):
    groups, _, windows, bins, _ = halves.shape
    every = groups * windows
    resident = pl.BlockSpec(memory_space=pltpu.VMEM)
    return pl.pallas_call(
        own_kernel,
        in_specs=[resident] * 2,
        out_specs=[resident] * 2,
        out_shape=[
            jax.ShapeDtypeStruct((bins, 2, OFFSETS, LANES), F32),
            jax.ShapeDtypeStruct((bins, 2 * every, LANES), BF16),
        ],
        scratch_shapes=[pltpu.VMEM(((every + 1) * PITCH, LANES), F32)] * 2,
        compiler_params=pltpu.CompilerParams(vmem_limit_bytes=20 * 2**20),
        cost_estimate=pl.CostEstimate(
            flops=2 * bins * 128 * 96 * 256,
            bytes_accessed=4 * halves.size + 4 * OFFSETS * 2 * bins * LANES,
            transcendentals=0,
        ),
        name="own_spectra",
    )(limit, halves)


def next_spectra(limit, own, later, after, begin, done):
    groups, windows, bins, _ = after.shape
    step = 16
    every = groups * windows
    resident = pl.BlockSpec(memory_space=pltpu.VMEM)
    anywhere = pl.BlockSpec(memory_space=pl.ANY)
    filled = [] if done is None else [done]
    return pl.pallas_call(
        functools.partial(next_kernel, begin),
        in_specs=[resident] * 4 + [anywhere] * len(filled),
        out_specs=anywhere,
        out_shape=jax.ShapeDtypeStruct((OFFSETS, 2, own.shape[0], LANES), F32),
        input_output_aliases={4: 0} if filled else {},
        scratch_shapes=[
            pltpu.VMEM(((every + 1) * PITCH, LANES), F32),
            pltpu.VMEM((bins // 8, 2, OFFSETS, 8, LANES), F32),
            pltpu.SemaphoreType.DMA((bins // 8, 2)),
        ],
        compiler_params=pltpu.CompilerParams(vmem_limit_bytes=20 * 2**20),
        cost_estimate=pl.CostEstimate(
            flops=2 * bins * 64 * 96 * 128,
            bytes_accessed=2 * after.size + 8 * OFFSETS * 2 * bins * LANES,
            transcendentals=0,
        ),
        name="next_spectra",
    )(limit, own, later, after, *filled)


def exchanged(blocks, axis):
    flat = blocks.reshape(blocks.shape[0], -1, LANES)
    flat = lax.all_to_all(flat, axis, split_axis=0, concat_axis=0, tiled=True)
    return flat.reshape(blocks.shape)


def body(down, back, records, channel_live, offset_limit):
    parts = lax.axis_size("fibre")
    groups = lax.axis_size("freq")
    sums = project(down, records, parts)
    sums = exchanged(sums, "fibre")
    halves = whiten(channel_live[None, :], back, sums, groups)
    halves = exchanged(halves, "freq")
    back_one = [(i, i - 1) for i in range(1, parts)]
    bounds = (0, 32, NB // groups)
    after = [
        lax.ppermute(halves[:, 0, :, low:high], "fibre", back_one)
        for low, high in zip(bounds, bounds[1:])
    ]
    limit = offset_limit[None, :]
    own, later = own_spectra(limit, halves)
    out = None
    for low, piece in zip(bounds, after):
        out = next_spectra(limit, own, later, piece, low, out)
    return out


def solution(mesh):
    down, back = make_tables(mesh.shape["fibre"])
    down = np.concatenate(split_pair(down))
    back = split_pair(back)[0]
    return jax.shard_map(
        functools.partial(body, down, back),
        mesh=mesh,
        in_specs=(P("freq", "fibre", None), P("fibre"), P("fibre")),
        out_specs=P(None, None, "freq", "fibre"),
        check_vma=False,
    )
```
